256 devices in a mesh: wide: 64 (over y, x_lo, z), lev: 4 (over x_hi, core).
Axes of the slice: x: 4 (x_hi: 2, x_lo: 2; x = x_hi * 2 + x_lo), y: 4, z: 8, core: 2. Of those that a mesh axis runs over, the one named last changes fastest.
Arguments:
- state_field: float32 [12, 1472, 1472], P('lev', 'wide'), may hold values from -8 to 8
- to_modes: float32 [12, 12], replicated, may hold values from -4 to 4
- from_modes: float32 [12, 12], replicated, may hold values from -4 to 4, as said below
- mode_depth: float32 [12], replicated, may hold values from 0.1 to 2000
Outputs:
- updated_field: float32 [12, 1472, 1472], P('lev', 'wide')
The draws below stay inside these ranges and needn't reach their ends.
Inputs may be any that keep to these rules, and one draw needn't show every extreme that they name: `from_modes`: the inverse of to_modes.
All inputs are finite; a program needn't handle non-finite values.
Results may differ from the reference program's by a relative error of at most 0.000094.
Values sent between devices are 32-bit elements; how exact they have to be, the bound alone decides.
A program may use at most 64 MiB of HBM per device.

```python
import math
import jax
import jax.numpy as jnp
from jax import lax

I = 1472
E = 64
K = 12
KT = 512


def mode_pair(key):
    noise = jax.random.truncated_normal(key, -3.0, 3.0, (K, K), jnp.float32)
    return jnp.eye(K, dtype=jnp.float32) + 0.25 / math.sqrt(K) * noise


def draw_to_modes(key, part):
    return mode_pair(jax.random.fold_in(key, 11))


def draw_from_modes(key, part):
    return jnp.linalg.inv(mode_pair(jax.random.fold_in(key, 11)))


def draw_state_field(key, part):
    first_key = jax.random.fold_in(jax.random.fold_in(key, 5), 0)
    return jax.random.truncated_normal(first_key, -6.0, 6.0, (K, I, I), jnp.float32)


def setup_inputs(seed: int = 0) -> dict:
    key_list = jax.random.split(jax.random.key(seed), 5)
    return {
        "state_field": draw_state_field(jax.random.fold_in(key_list[4], 71), 0),
        "to_modes": draw_to_modes(jax.random.fold_in(key_list[4], 71), 0),
        "from_modes": draw_from_modes(jax.random.fold_in(key_list[4], 71), 0),
        "mode_depth": jnp.clip(jnp.exp(jax.random.uniform(key_list[3], (K,), jnp.float32, math.log(0.1), math.log(2000.0))), 0.1, 2000.0),
    }


def blend_weights(fraction):
    square = fraction * fraction
    cubed = square * fraction
    return (2.0 * cubed - 3.0 * square + 1.0, cubed - 2.0 * square + fraction, -2.0 * cubed + 3.0 * square, cubed - square)

def hermite_mix(start_val, start_slope, end_val, end_slope, weights):
    return weights[0] * end_val + weights[1] * end_slope + weights[2] * start_val + weights[3] * start_slope

def extend_cols(sub_block, extra):
    fraction = (jnp.arange(extra, dtype=jnp.float32) + 1.0) / (extra + 1.0)
    weights = blend_weights(fraction)
    end_val = sub_block[..., -1:]
    end_slope = sub_block[..., -1:] - sub_block[..., -2:-1]
    start_val = sub_block[..., :1]
    start_slope = sub_block[..., 1:2] - sub_block[..., :1]
    added = hermite_mix(start_val, start_slope, end_val, end_slope, weights)
    return jnp.concatenate([sub_block, added], axis=-1)

def laplace(waves, length):
    sines = jnp.sin(math.pi / length * waves.astype(jnp.float32))
    return 4.0 * sines * sines

def hartley(values, axis):
    spectral = jnp.fft.fft(values, axis=axis)
    return jnp.real(spectral) - jnp.imag(spectral)

def reference(state_field, to_modes, from_modes, mode_depth):
    length = I + E

    def forward(one_level):
        tall = jnp.swapaxes(extend_cols(jnp.swapaxes(one_level, 0, 1), E), 0, 1)
        extended = extend_cols(tall, E)
        return hartley(hartley(extended, 0), 1)
    spectra = lax.map(forward, state_field)
    indices = jnp.arange(length, dtype=jnp.int32)
    magnitude = jnp.minimum(indices, length - indices)
    lap_line = laplace(indices, length)
    inside = magnitude[:, None] * magnitude[:, None] + magnitude[None, :] * magnitude[None, :] < KT * KT
    keep_mask = inside.astype(jnp.float32)
    lap_sum = lap_line[:, None] + lap_line[None, :]
    mode_values = jnp.einsum('ml,lyx->myx', to_modes, spectra, precision=lax.Precision.HIGHEST)
    solved = mode_values * keep_mask / (1.0 + mode_depth[:, None, None] * lap_sum)
    mixed_levels = jnp.einsum('lm,myx->lyx', from_modes, solved, precision=lax.Precision.HIGHEST)

    def inverse(one_level):
        return (hartley(hartley(one_level, 0), 1) / (length * length))[:I, :I]
    return lax.map(inverse, mixed_levels)
```

```python
import functools
import math

import jax
import jax.numpy as jnp
import ml_dtypes
import numpy as np
from jax import lax
from jax.experimental import pallas as pl
from jax.experimental.pallas import tpu as pltpu
from jax.sharding import PartitionSpec as P

I = 1472
E = 64
K = 12
KT = 512
N = I + E
W = 2 * KT
RING = 8
CROSS = 8
LEV = 4
LOC = 3
ROWS = 23
PAD = 24
PEERS = CROSS * LEV
COLS = 4
M = K * COLS
MESH = pl.DeviceIdType.MESH
F32 = jnp.float32
BF16 = jnp.bfloat16


def wave_of(position):
    return np.where(position < KT, position, position + N - W)


def pair(table):
    high = table.astype(ml_dtypes.bfloat16)
    low = (table - high.astype(np.float64)).astype(ml_dtypes.bfloat16)
    depth, width = table.shape
    blocks = width // 128
    both = np.stack([high.reshape(depth, blocks, 128), low.reshape(depth, blocks, 128)], axis=2)
    return np.ascontiguousarray(both.transpose(1, 0, 2, 3).reshape(blocks, depth, 256))


@functools.lru_cache(maxsize=None)
def tables():
    position = np.arange(W)
    waves = wave_of(position)
    angle = 2.0 * np.pi / N * ((np.arange(N)[:, None] * waves[None, :]) % N)
    cas = np.cos(angle) + np.sin(angle)
    f = (np.arange(E) + 1.0) / (E + 1.0)
    h00, h10 = 2 * f**3 - 3 * f**2 + 1, f**3 - 2 * f**2 + f
    h01, h11 = -2 * f**3 + 3 * f**2, f**3 - f**2
    forward = cas[:I].copy()
    forward[I - 1] += (h00 + h10) @ cas[I:]
    forward[I - 2] -= h10 @ cas[I:]
    forward[0] += (h01 - h11) @ cas[I:]
    forward[1] += h11 @ cas[I:]
    inverse = cas[:I].T / N

    fx = np.zeros((N, W))
    fx[:I] = forward
    lane = np.arange(256)
    ring, row = lane // PAD, lane % PAD
    good = (lane < RING * PAD) & (row < ROWS)
    source = ROWS * (np.arange(CROSS)[:, None] * RING + ring[None, :]) + row[None, :]
    source = np.where(good[None, :], source, 0).reshape(-1)
    good = np.tile(good, CROSS)
    fy = np.where(good[:, None], forward[source], 0.0)
    iy = np.where(good[None, :], inverse[:, source], 0.0)
    ix = np.zeros((W, N))
    ix[:, :I] = inverse
    magnitude = np.minimum(waves, N - waves)
    lap = 4.0 * np.sin(np.pi * waves / N) ** 2
    line = np.zeros((8, W), np.float32)
    line[0], line[1] = lap, magnitude
    return pair(fx), pair(fy), pair(iy), pair(ix), line


def split(value):
    high = value.astype(BF16)
    return high, (value - high.astype(F32)).astype(BF16)


def total(product, rows):
    return (
        (product[rows:, 128:] + product[:rows, 128:]) + product[rows:, :128]
    ) + product[:rows, :128]


def kernel(
    x_ref, to_ref, from_ref, depth_ref, line_ref, fx_hbm, fy_hbm, iy_hbm, ix_hbm, out_ref,
    fx, fy, iy, ix, xf, xs, ys, ms, zs,
    send_a, recv_a, send_b, recv_b, send_c, recv_c, send_d, recv_d,
    fx_sem, table_sem, sa_sem, ra_sem, sb_sem, rb_sem, sc_sem, rc_sem, sd_sem, rd_sem,
):
    wide = lax.axis_index("wide")
    lev = lax.axis_index("lev")
    ring = lax.rem(wide, RING)
    cross = lax.div(wide, RING)
    me = cross * LEV + lev

    def ring_id(z):
        return {"wide": cross * RING + z, "lev": lev}

    def peer_id(s):
        return {"wide": lax.div(s, LEV) * RING + ring, "lev": lax.rem(s, LEV)}

    order = [lax.rem(ring + step, RING) for step in (4, 3, 5, 2, 6, 1, 7, 0)]

    fx_copies = []
    for n, z in enumerate(order):
        copy = pltpu.make_async_copy(fx_hbm.at[z], fx.at[n], fx_sem.at[n])
        copy.start()
        fx_copies.append(copy)
    rest = [
        pltpu.make_async_copy(source, target, table_sem.at[n])
        for n, (source, target) in enumerate(((fy_hbm, fy), (iy_hbm, iy), (ix_hbm, ix)))
    ]

    barrier = pltpu.get_barrier_semaphore()
    for z in order[:-1]:
        pl.semaphore_signal(barrier, inc=1, device_id=ring_id(z), device_id_type=MESH)

    @pl.loop(1, PEERS)
    def _(step):
        s = lax.rem(me + step, PEERS)
        pl.semaphore_signal(barrier, inc=1, device_id=peer_id(s), device_id_type=MESH)

    for copy in rest:
        copy.start()

    xf[...] = jnp.zeros_like(xf)
    for l in range(LOC):
        xf[l * PAD : l * PAD + ROWS, :I] = x_ref[l]
    high, low = split(xf[...])
    xs[:80] = high
    xs[80:] = low

    pl.semaphore_wait(barrier, RING - 1 + PEERS - 1)

    def ring_copy(z, l):
        rows = pl.ds(l * PAD, PAD)
        return pltpu.make_async_remote_copy(
            src_ref=send_a.at[z, rows],
            dst_ref=recv_a.at[l, ring],
            send_sem=sa_sem,
            recv_sem=ra_sem.at[l],
            device_id=ring_id(z),
            device_id_type=MESH,
        )

    for n, z in enumerate(order):
        fx_copies[n].wait()
        block = total(jnp.dot(xs[...], fx[n], preferred_element_type=F32), 80)[: LOC * PAD]
        if n < RING - 1:
            send_a[z] = block
            ring_copy(z, 0).start()
        else:
            for l in range(LOC):
                recv_a[l, ring] = block[l * PAD : (l + 1) * PAD]
    for l in range(1, LOC):
        for z in order[:-1]:
            ring_copy(z, l).start()

    row = lax.broadcasted_iota(jnp.int32, (M, 1), 0)
    level_of_row = lax.div(lax.rem(row, 16), COLS) * LOC + lax.div(row, 16)
    pick = (level_of_row == lax.broadcasted_iota(jnp.int32, (M, K), 1)).astype(F32)
    same = (
        lax.rem(row, COLS) == lax.rem(lax.broadcasted_iota(jnp.int32, (M, M), 1), COLS)
    ).astype(F32)

    def expand(small):
        tall = jnp.dot(pick, small, preferred_element_type=F32, precision=lax.Precision.HIGHEST)
        full = lax.dot_general(
            tall, pick, (((1,), (1,)), ((), ())),
            preferred_element_type=F32, precision=lax.Precision.HIGHEST,
        )
        return full * same

    to_big = expand(to_ref[...])
    from_big = expand(from_ref[...])
    depth = jnp.sum(pick * depth_ref[...], axis=1, keepdims=True)
    column = ring * 128 + me * COLS + lax.rem(row, COLS)
    hit = lax.broadcasted_iota(jnp.int32, (M, W), 1) == column
    lap_q = jnp.sum(jnp.where(hit, line_ref[0:1], 0.0), axis=1, keepdims=True)
    mag_q = jnp.sum(jnp.where(hit, line_ref[1:2], 0.0), axis=1, keepdims=True)
    top = lax.broadcasted_iota(jnp.int32, (8, 128), 0) < COLS

    def cross_copy(l, s):
        return pltpu.make_async_remote_copy(
            src_ref=send_b.at[l, s],
            dst_ref=recv_b.at[l, me],
            send_sem=sb_sem,
            recv_sem=rb_sem.at[l],
            device_id=peer_id(s),
            device_id_type=MESH,
        )

    def bulk(ref, sem):
        return pltpu.make_async_copy(ref, ref, sem)

    for l in range(LOC):
        bulk(recv_a.at[l, pl.ds(0, RING - 1)], ra_sem.at[l]).wait()
        rows = recv_a[l].reshape(RING * PAD, 128)
        first = rows[:128].T
        second = jnp.concatenate([rows[128:], jnp.zeros((64, 128), F32)], axis=0).T
        for g in range(PEERS // 2):
            a, b = first[8 * g : 8 * g + 8], second[8 * g : 8 * g + 8]
            send_b[l, 2 * g] = jnp.where(top, a, pltpu.roll(b, 4, 0))
            send_b[l, 2 * g + 1] = jnp.where(top, pltpu.roll(a, 4, 0), b)
        recv_b[l, me] = send_b[l, me]

        @pl.loop(1, PEERS)
        def _(step):
            cross_copy(l, lax.rem(me + step, PEERS)).start()

    for l in range(LOC):
        bulk(recv_b.at[l, pl.ds(0, PEERS - 1)], rb_sem.at[l]).wait()
        for c in range(CROSS):
            v = [recv_b[l, c * LEV + k] for k in range(LEV)]
            a = [jnp.where(top, v[k], pltpu.roll(v[k + 1], 4, 0)) for k in (0, 2)]
            b = [jnp.where(top, pltpu.roll(v[k], 4, 0), v[k + 1]) for k in (0, 2)]
            for t, half in enumerate((a, b)):
                high, low = split(jnp.concatenate(half, axis=0))
                lanes = slice((2 * c + t) * 128, (2 * c + t + 1) * 128)
                ys[16 * l : 16 * l + 16, lanes] = high
                ys[M + 16 * l : M + 16 * l + 16, lanes] = low

    rest[0].wait()

    @pl.loop(0, RING)
    def _(j):
        lanes = pl.ds(pl.multiple_of(j * 128, 128), 128)
        spectrum = total(jnp.dot(ys[...], fy[j], preferred_element_type=F32), M)
        modes = jnp.dot(to_big, spectrum, preferred_element_type=F32, precision=lax.Precision.HIGHEST)
        lap_p = line_ref[0:1, lanes]
        mag_p = line_ref[1:2, lanes]
        keep = (mag_p * mag_p + mag_q * mag_q < float(KT * KT)).astype(F32)
        solved = modes * keep / (1.0 + depth * (lap_p + lap_q))
        mixed = jnp.dot(from_big, solved, preferred_element_type=F32, precision=lax.Precision.HIGHEST)
        high, low = split(mixed)
        ms[:M, lanes] = high
        ms[M:, lanes] = low

    rest[1].wait()

    def back_copy(l, s):
        return pltpu.make_async_remote_copy(
            src_ref=send_c.at[l, s],
            dst_ref=recv_c.at[l, me],
            send_sem=sc_sem,
            recv_sem=rc_sem.at[l],
            device_id=peer_id(s),
            device_id_type=MESH,
        )

    @pl.loop(0, CROSS)
    def _(step):
        c = lax.rem(cross + 1 + step, CROSS)
        half = [
            total(jnp.dot(ms[...], iy[2 * c + t], preferred_element_type=F32), M)
            for t in range(2)
        ]
        for l in range(LOC):
            for k in (0, 2):
                at = 16 * l + 4 * k
                a, b = half[0][at : at + 8], half[1][at : at + 8]
                send_c[l, c * LEV + k] = jnp.where(top, a, pltpu.roll(b, 4, 0))
                send_c[l, c * LEV + k + 1] = jnp.where(top, pltpu.roll(a, 4, 0), b)

        @pl.when(step < CROSS - 1)
        def _():
            for k in range(LEV):
                back_copy(0, c * LEV + k).start()

    for k in range(1, LEV):
        back_copy(0, cross * LEV + lax.rem(lev + k, LEV)).start()
    for l in range(LOC):
        recv_c[l, me] = send_c[l, me]
        if l:

            @pl.loop(1, PEERS)
            def _(step):
                back_copy(l, lax.rem(me + step, PEERS)).start()

    def home_copy(l, z):
        return pltpu.make_async_remote_copy(
            src_ref=send_d.at[l, z],
            dst_ref=recv_d.at[ring, l],
            send_sem=sd_sem,
            recv_sem=rd_sem,
            device_id=ring_id(z),
            device_id_type=MESH,
        )

    for l in range(LOC):
        bulk(recv_c.at[l, pl.ds(0, PEERS - 1)], rc_sem.at[l]).wait()
        first, second = [], []
        for g in range(PEERS // 2):
            a, b = recv_c[l, 2 * g], recv_c[l, 2 * g + 1]
            first.append(jnp.where(top, a, pltpu.roll(b, 4, 0)))
            second.append(jnp.where(top, pltpu.roll(a, 4, 0), b))
        rows = jnp.concatenate(
            [jnp.concatenate(first, axis=0).T, jnp.concatenate(second, axis=0).T[:64]], axis=0
        )
        send_d[l] = rows.reshape(RING, PAD, 128)
        recv_d[ring, l] = send_d[l, ring]
        for z in order[:-1]:
            home_copy(l, z).start()

    bulk(recv_d.at[pl.ds(0, RING - 1)], rd_sem).wait()
    for z in range(RING):
        block = recv_d[z].reshape(LOC * PAD, 128)
        high, low = split(jnp.concatenate([block, jnp.zeros((8, 128), F32)], axis=0))
        zs[:80, z * 128 : (z + 1) * 128] = high
        zs[80:, z * 128 : (z + 1) * 128] = low

    rest[2].wait()
    for j in range(N // 128):
        field = total(jnp.dot(zs[...], ix[j], preferred_element_type=F32), 80)
        width = min(128, I - j * 128)
        for l in range(LOC):
            out_ref[l, :, j * 128 : j * 128 + width] = field[l * PAD : l * PAD + ROWS, :width]

    bulk(send_a.at[pl.ds(0, RING - 1)], sa_sem).wait()
    for l in range(LOC):
        bulk(send_b.at[l, pl.ds(0, PEERS - 1)], sb_sem).wait()
        bulk(send_c.at[l, pl.ds(0, PEERS - 1)], sc_sem).wait()
        bulk(send_d.at[l, pl.ds(0, RING - 1)], sd_sem).wait()


def shards(state_field, to_modes, from_modes, mode_depth):
    fx, fy, iy, ix, line = (jnp.asarray(table) for table in tables())
    vmem = pl.BlockSpec(memory_space=pltpu.VMEM)
    hbm = pl.BlockSpec(memory_space=pl.ANY)
    dma = pltpu.SemaphoreType.DMA
    return pl.pallas_call(
        kernel,
        out_shape=jax.ShapeDtypeStruct((LOC, ROWS, I), F32),
        in_specs=[vmem] * 5 + [hbm] * 4,
        out_specs=vmem,
        scratch_shapes=[
            pltpu.VMEM(fx.shape, BF16),
            pltpu.VMEM(fy.shape, BF16),
            pltpu.VMEM(iy.shape, BF16),
            pltpu.VMEM(ix.shape, BF16),
            pltpu.VMEM((80, N), F32),
            pltpu.VMEM((160, N), BF16),
            pltpu.VMEM((2 * M, CROSS * 256), BF16),
            pltpu.VMEM((2 * M, W), BF16),
            pltpu.VMEM((160, W), BF16),
            pltpu.VMEM((RING, LOC * PAD, 128), F32),
            pltpu.VMEM((LOC, RING, PAD, 128), F32),
            pltpu.VMEM((LOC, PEERS, 8, 128), F32),
            pltpu.VMEM((LOC, PEERS, 8, 128), F32),
            pltpu.VMEM((LOC, PEERS, 8, 128), F32),
            pltpu.VMEM((LOC, PEERS, 8, 128), F32),
            pltpu.VMEM((LOC, RING, PAD, 128), F32),
            pltpu.VMEM((RING, LOC, PAD, 128), F32),
            dma((RING,)),
            dma((3,)),
            dma,
            dma((LOC,)),
            dma,
            dma((LOC,)),
            dma,
            dma((LOC,)),
            dma,
            dma,
        ],
        compiler_params=pltpu.CompilerParams(
            collective_id=0, has_side_effects=True, vmem_limit_bytes=56 * 2**20
        ),
        cost_estimate=pl.CostEstimate(flops=4 * 10**9, bytes_accessed=32 * 10**6, transcendentals=0),
    )(state_field, to_modes, from_modes, mode_depth.reshape(1, K), line, fx, fy, iy, ix)


def solution(mesh):
    assert dict(mesh.shape) == {"wide": RING * CROSS, "lev": LEV}
    placed = (P("lev", "wide", None), P(), P(), P())
    return jax.shard_map(
        shards, mesh=mesh, in_specs=placed, out_specs=P("lev", "wide", None), check_vma=False
    )
```

```python
import functools
import math

import jax
import jax.numpy as jnp
import ml_dtypes
import numpy as np
from jax import lax
from jax.experimental import pallas as pl
from jax.experimental.pallas import tpu as pltpu
from jax.sharding import PartitionSpec as P

I = 1472
E = 64
K = 12
KT = 512
N = I + E
W = 2 * KT
RING = 8
WIDE = 64
LEV = 4
CHIPS = 128
LOC = 3
ROWS = 23
PAD = 24
COLS = 4
LAST = 5
M = K * COLS
MESH = pl.DeviceIdType.MESH
F32 = jnp.float32
BF16 = jnp.bfloat16


def wave_of(position):
    return np.where(position < KT, position, position + N - W)


def pair(table):
    high = table.astype(ml_dtypes.bfloat16)
    low = (table - high.astype(np.float64)).astype(ml_dtypes.bfloat16)
    depth, width = table.shape
    blocks = width // 128
    both = np.stack([high.reshape(depth, blocks, 128), low.reshape(depth, blocks, 128)], axis=2)
    return np.ascontiguousarray(both.transpose(1, 0, 2, 3).reshape(blocks, depth, 256))


@functools.lru_cache(maxsize=None)
def tables():
    position = np.arange(W)
    waves = wave_of(position)
    angle = 2.0 * np.pi / N * ((np.arange(N)[:, None] * waves[None, :]) % N)
    cas = np.cos(angle) + np.sin(angle)
    f = (np.arange(E) + 1.0) / (E + 1.0)
    h00, h10 = 2 * f**3 - 3 * f**2 + 1, f**3 - 2 * f**2 + f
    h01, h11 = -2 * f**3 + 3 * f**2, f**3 - f**2
    forward = cas[:I].copy()
    forward[I - 1] += (h00 + h10) @ cas[I:]
    forward[I - 2] -= h10 @ cas[I:]
    forward[0] += (h01 - h11) @ cas[I:]
    forward[1] += h11 @ cas[I:]
    inverse = cas[:I].T / N

    fx = np.zeros((N, W))
    fx[:I] = forward
    index, device = np.arange(N) // WIDE, np.arange(N) % WIDE
    good = index < ROWS
    source = np.where(good, ROWS * device + index, 0)
    fy = np.where(good[:, None], forward[source], 0.0)
    iy = np.where(good[None, :], inverse[:, source], 0.0)
    ix = np.zeros((W, N))
    ix[:, :I] = inverse
    ix = np.stack([pair(ix[: W // 2]), pair(ix[W // 2 :])])
    magnitude = np.minimum(waves, N - waves)
    lap = 4.0 * np.sin(np.pi * waves / N) ** 2
    line = np.zeros((8, W), np.float32)
    line[0], line[1] = lap, magnitude
    return pair(fx), pair(fy), pair(iy), ix, line


def split(value):
    high = value.astype(BF16)
    return high, (value - high.astype(F32)).astype(BF16)


def total(product, rows):
    return (
        (product[rows:, 128:] + product[:rows, 128:]) + product[rows:, :128]
    ) + product[:rows, :128]


def split_three(value):
    high, rest = value.astype(BF16), value
    rest = rest - high.astype(F32)
    middle = rest.astype(BF16)
    return high, middle, (rest - middle.astype(F32)).astype(BF16)


def kernel(
    x_ref, to_ref, from_ref, depth_ref, line_ref, fx_hbm, fy_hbm, iy_hbm, ix_hbm, out_ref,
    fx, fy, iy, ix, xf, xs, ys, qs, ms, zs, part,
    swap_x, spec_x, send_a, recv_a, mid_a, mid_b, send_b, recv_b, home, other,
    fx_sem, table_sem, swap_sem, s1_sem, s2_sem, r2_sem, s3_sem, r3_sem, all_sem,
):
    wide = lax.axis_index("wide")
    lev = lax.axis_index("lev")
    core = lev & 1
    half = lev >> 1
    ring = wide & (RING - 1)
    me = half * WIDE + wide
    partner = {"wide": wide, "lev": lev ^ 1}

    def chip(s):
        return {"wide": s & (WIDE - 1), "lev": ((s >> 6) << 1) + core}

    def across(q):
        return chip((q << 3) + ring)

    cross = me >> 3

    blocks = [(core ^ 1) * COLS + c for c in range(COLS)] + [core * COLS + c for c in range(COLS)]
    fx_copies = []
    for n, block in enumerate(blocks):
        copy = pltpu.make_async_copy(fx_hbm.at[block], fx.at[n], fx_sem.at[n])
        copy.start()
        fx_copies.append(copy)
    rest = [
        pltpu.make_async_copy(source, target, table_sem.at[n])
        for n, (source, target) in enumerate(((fy_hbm, fy), (iy_hbm, iy), (ix_hbm, ix)))
    ]

    barrier = pltpu.get_barrier_semaphore()
    for step in range(1, RING):
        z = (ring + step) & (RING - 1)
        pl.semaphore_signal(
            barrier, inc=1, device_id=chip(me - ring + z), device_id_type=MESH
        )
    for step in range(1, 16):
        pl.semaphore_signal(
            barrier, inc=1, device_id=across((cross + step) & 15), device_id_type=MESH
        )
    pl.semaphore_signal(barrier, inc=1, device_id=partner, device_id_type=MESH)

    for copy in rest:
        copy.start()

    xf[...] = jnp.zeros_like(xf)
    for l in range(LOC):
        xf[l * PAD : l * PAD + ROWS, :I] = x_ref[l]
    high, low = split(xf[...])
    xs[:80] = high
    xs[80:] = low

    def swap_copy(c):
        return pltpu.make_async_remote_copy(
            src_ref=swap_x.at[c],
            dst_ref=spec_x.at[pl.ds(core * LOC, LOC), c],
            send_sem=s1_sem,
            recv_sem=swap_sem,
            device_id=partner,
            device_id_type=MESH,
        )

    for n in range(2 * COLS):
        fx_copies[n].wait()
        block = total(jnp.dot(xs[...], fx[n], preferred_element_type=F32), 80)[: LOC * PAD]
        block = block.reshape(LOC, PAD, 128)
        if n < COLS:
            swap_x[n] = block
            if n == 0:
                pl.semaphore_wait(barrier, RING - 1 + 15 + 1)
                for step in range(1, 16):
                    pl.semaphore_signal(
                        all_sem, inc=1, device_id=across((cross + step) & 15), device_id_type=MESH
                    )
            swap_copy(n).start()
        else:
            for l in range(LOC):
                spec_x[core * LOC + l, n - COLS] = block[l]

    def bulk(ref, sem):
        return pltpu.make_async_copy(ref, ref, sem)

    bulk(spec_x.at[pl.ds(0, LOC)], swap_sem).wait()

    def pack(rows, buffer):
        last = rows(LAST)
        for l in range(LAST):
            tail = last[32 * l : 32 * l + 32] if l < 3 else jnp.zeros((32, 128), F32)
            buffer[pl.ds(l, CHIPS, stride=8), :] = jnp.concatenate([rows(l), tail], axis=0).T

    def unpack(buffer, store):
        for l in range(LAST):
            rows = buffer[pl.ds(l, CHIPS, stride=8), :].T
            store(l, 0, rows[:96])
            if l < 3:
                store(LAST, 32 * l, rows[96:])

    pack(lambda l: spec_x[l].reshape(96, 128), send_a)

    def exchange(source, target, send_sem, recv_sem):
        def copy(s):
            return pltpu.make_async_remote_copy(
                src_ref=source.at[pl.ds(pl.multiple_of(s * 8, 8), LAST)],
                dst_ref=target.at[pl.ds(pl.multiple_of(me * 8, 8), LAST)],
                send_sem=send_sem,
                recv_sem=recv_sem,
                device_id=chip(s),
                device_id_type=MESH,
            )

        @pl.loop(1, CHIPS)
        def _(step):
            copy((me + step) & (CHIPS - 1)).start()

        own = pl.ds(pl.multiple_of(me * 8, 8), 8)
        target[own, :] = source[own, :]

    def arrived(buffer, sem):
        bulk(buffer.at[pl.ds(0, (CHIPS - 1) * LAST)], sem).wait()

    pl.semaphore_wait(all_sem, 15)
    exchange(send_a, recv_a, s2_sem, r2_sem)

    row = lax.broadcasted_iota(jnp.int32, (M, 1), 0)
    pick = ((row >> 2) == lax.broadcasted_iota(jnp.int32, (M, K), 1)).astype(F32)
    turn = lax.broadcasted_iota(jnp.int32, (6 * M, 1), 0)
    turn = lax.rem(turn, M) >> 2
    pick_six = (turn == lax.broadcasted_iota(jnp.int32, (6 * M, K), 1)).astype(F32)
    lane = lax.broadcasted_iota(jnp.int32, (M, 6 * M), 1)
    same = (row & 3) == (lane & 3)

    def expand(small):
        tall = jnp.dot(pick, small, preferred_element_type=F32, precision=lax.Precision.HIGHEST)
        full = lax.dot_general(
            tall, pick_six, (((1,), (1,)), ((), ())),
            preferred_element_type=F32, precision=lax.Precision.HIGHEST,
        )
        full = jnp.where(same, full, 0.0)
        high = full.astype(BF16).astype(F32)
        middle = (full - high).astype(BF16).astype(F32)
        low = full - high - middle
        return jnp.where(lane < 3 * M, high, jnp.where(lane < 5 * M, middle, low)).astype(BF16)

    to_big = expand(to_ref[...])
    from_big = expand(from_ref[...])
    depth = jnp.sum(pick * depth_ref[...], axis=1, keepdims=True)
    column = core * (W // 2) + (row & 3) * CHIPS + me
    hit = lax.broadcasted_iota(jnp.int32, (M, W), 1) == column
    lap_q = jnp.sum(jnp.where(hit, line_ref[0:1], 0.0), axis=1, keepdims=True)
    mag_q = jnp.sum(jnp.where(hit, line_ref[1:2], 0.0), axis=1, keepdims=True)
    left = lax.broadcasted_iota(jnp.int32, (M // 2, 128), 1) < WIDE

    def mix(matrix, value):
        high, middle, low = split_three(value)
        for n, piece in enumerate((high, middle, low, high, middle, high)):
            qs[n * M : (n + 1) * M] = piece
        return jnp.dot(matrix, qs[...], preferred_element_type=F32)

    arrived(recv_a, r2_sem)

    def store_a(l, at, rows):
        mid_a[l * 96 + at : l * 96 + at + rows.shape[0]] = rows

    unpack(recv_a, store_a)
    for t in range(PAD // 2):
        a = mid_a[pl.ds(2 * t, M // 2, stride=PAD), :]
        b = mid_a[pl.ds(2 * t + 1, M // 2, stride=PAD), :]
        first = jnp.where(left, a, pltpu.roll(b, WIDE, 1))
        second = jnp.where(left, pltpu.roll(a, WIDE, 1), b)
        high, low = split(jnp.concatenate([first, second], axis=0))
        ys[:M, t * 128 : t * 128 + 128] = high
        ys[M:, t * 128 : t * 128 + 128] = low

    rest[0].wait()

    @pl.loop(0, W // 256)
    def _(j):
        lanes = pl.ds(pl.multiple_of(j * 256, 256), 256)
        spectrum = jnp.concatenate(
            [
                total(jnp.dot(ys[...], fy[2 * j + n], preferred_element_type=F32), M)
                for n in range(2)
            ],
            axis=1,
        )
        modes = mix(to_big, spectrum)
        lap_p = line_ref[0:1, lanes]
        mag_p = line_ref[1:2, lanes]
        keep = (mag_p * mag_p + mag_q * mag_q < float(KT * KT)).astype(F32)
        solved = modes * keep / (1.0 + depth * (lap_p + lap_q))
        high, low = split(mix(from_big, solved))
        ms[:M, lanes] = high
        ms[M:, lanes] = low

    rest[1].wait()
    for t in range(PAD // 2):
        value = total(jnp.dot(ms[...], iy[t], preferred_element_type=F32), M)
        first, second = value[: M // 2], value[M // 2 :]
        mid_b[pl.ds(2 * t, M // 2, stride=PAD), :] = jnp.where(
            left, first, pltpu.roll(second, WIDE, 1)
        )
        mid_b[pl.ds(2 * t + 1, M // 2, stride=PAD), :] = jnp.where(
            left, pltpu.roll(first, WIDE, 1), second
        )
    pack(lambda l: mid_b[l * 96 : l * 96 + 96], send_b)
    exchange(send_b, recv_b, s3_sem, r3_sem)
    rest[2].wait()
    arrived(recv_b, r3_sem)

    def store_b(l, at, rows):
        home[l, at : at + rows.shape[0]] = rows

    unpack(recv_b, store_b)
    back = pltpu.make_async_remote_copy(
        src_ref=home.at[pl.ds((core ^ 1) * LOC, LOC)],
        dst_ref=other,
        send_sem=table_sem.at[3],
        recv_sem=table_sem.at[4],
        device_id=partner,
        device_id_type=MESH,
    )
    back.start()

    def gather(level):
        for c in range(COLS):
            rows = [level(l)[PAD * c : PAD * c + PAD] for l in range(LOC)]
            high, low = split(jnp.concatenate(rows + [jnp.zeros((8, 128), F32)], axis=0))
            zs[:80, c * 128 : c * 128 + 128] = high
            zs[80:, c * 128 : c * 128 + 128] = low

    gather(lambda l: home[core * LOC + l])
    for j in range(N // 128):
        part[:, j * 128 : j * 128 + 128] = total(
            jnp.dot(zs[...], ix[core, j], preferred_element_type=F32), 80
        )
    back.wait_recv()
    gather(lambda l: other[l])
    for j in range(N // 128):
        field = total(jnp.dot(zs[...], ix[core ^ 1, j], preferred_element_type=F32), 80)
        field = field + part[:, j * 128 : j * 128 + 128]
        width = min(128, I - j * 128)
        for l in range(LOC):
            out_ref[l, :, j * 128 : j * 128 + width] = field[l * PAD : l * PAD + ROWS, :width]

    bulk(swap_x, s1_sem).wait()
    arrived(send_a, s2_sem)
    arrived(send_b, s3_sem)
    back.wait_send()


def shards(state_field, to_modes, from_modes, mode_depth):
    fx, fy, iy, ix, line = (jnp.asarray(table) for table in tables())
    vmem = pl.BlockSpec(memory_space=pltpu.VMEM)
    hbm = pl.BlockSpec(memory_space=pl.ANY)
    dma = pltpu.SemaphoreType.DMA
    return pl.pallas_call(
        kernel,
        out_shape=jax.ShapeDtypeStruct((LOC, ROWS, I), F32),
        in_specs=[vmem] * 5 + [hbm] * 4,
        out_specs=vmem,
        scratch_shapes=[
            pltpu.VMEM(fx.shape, BF16),
            pltpu.VMEM(fy.shape, BF16),
            pltpu.VMEM(iy.shape, BF16),
            pltpu.VMEM(ix.shape, BF16),
            pltpu.VMEM((80, N), F32),
            pltpu.VMEM((160, N), BF16),
            pltpu.VMEM((2 * M, N), BF16),
            pltpu.VMEM((6 * M, 256), BF16),
            pltpu.VMEM((2 * M, W), BF16),
            pltpu.VMEM((160, W // 2), BF16),
            pltpu.VMEM((80, N), F32),
            pltpu.VMEM((COLS, LOC, PAD, 128), F32),
            pltpu.VMEM((2 * LOC, COLS, PAD, 128), F32),
            pltpu.VMEM((8 * CHIPS, 128), F32),
            pltpu.VMEM((8 * CHIPS, 128), F32),
            pltpu.VMEM((2 * LOC * 96, 128), F32),
            pltpu.VMEM((2 * LOC * 96, 128), F32),
            pltpu.VMEM((8 * CHIPS, 128), F32),
            pltpu.VMEM((8 * CHIPS, 128), F32),
            pltpu.VMEM((2 * LOC, 96, 128), F32),
            pltpu.VMEM((LOC, 96, 128), F32),
            dma((2 * COLS,)),
            dma((5,)),
            dma,
            dma,
            dma,
            dma,
            dma,
            dma,
            pltpu.SemaphoreType.REGULAR,
        ],
        compiler_params=pltpu.CompilerParams(
            collective_id=0, has_side_effects=True, vmem_limit_bytes=56 * 2**20
        ),
        cost_estimate=pl.CostEstimate(flops=4 * 10**9, bytes_accessed=27 * 10**6, transcendentals=0),
    )(state_field, to_modes, from_modes, mode_depth.reshape(1, K), line, fx, fy, iy, ix)


def solution(mesh):
    assert dict(mesh.shape) == {"wide": WIDE, "lev": LEV}
    placed = (P("lev", "wide", None), P(), P(), P())
    return jax.shard_map(
        shards, mesh=mesh, in_specs=placed, out_specs=P("lev", "wide", None), check_vma=False
    )
```

```python
import functools
import math

import jax
import jax.numpy as jnp
import ml_dtypes
import numpy as np
from jax import lax
from jax.experimental import pallas as pl
from jax.experimental.pallas import tpu as pltpu
from jax.sharding import PartitionSpec as P

I = 1472
E = 64
K = 12
KT = 512
N = I + E
W = 2 * KT
RING = 8
WIDE = 64
LEV = 4
CHIPS = 128
LOC = 3
ROWS = 23
PAD = 24
COLS = 4
LAST = 5
M = K * COLS
MESH = pl.DeviceIdType.MESH
F32 = jnp.float32
BF16 = jnp.bfloat16


def wave_of(position):
    return np.where(position < KT, position, position + N - W)


def pair(table):
    high = table.astype(ml_dtypes.bfloat16)
    low = (table - high.astype(np.float64)).astype(ml_dtypes.bfloat16)
    depth, width = table.shape
    blocks = width // 128
    both = np.stack([high.reshape(depth, blocks, 128), low.reshape(depth, blocks, 128)], axis=2)
    return np.ascontiguousarray(both.transpose(1, 0, 2, 3).reshape(blocks, depth, 256))


@functools.lru_cache(maxsize=None)
def tables():
    position = np.arange(W)
    waves = wave_of(position)
    angle = 2.0 * np.pi / N * ((np.arange(N)[:, None] * waves[None, :]) % N)
    cas = np.cos(angle) + np.sin(angle)
    f = (np.arange(E) + 1.0) / (E + 1.0)
    h00, h10 = 2 * f**3 - 3 * f**2 + 1, f**3 - 2 * f**2 + f
    h01, h11 = -2 * f**3 + 3 * f**2, f**3 - f**2
    forward = cas[:I].copy()
    forward[I - 1] += (h00 + h10) @ cas[I:]
    forward[I - 2] -= h10 @ cas[I:]
    forward[0] += (h01 - h11) @ cas[I:]
    forward[1] += h11 @ cas[I:]
    inverse = cas[:I].T / N

    fx = np.zeros((N, W))
    fx[:I] = forward
    index, device = np.arange(N) // WIDE, np.arange(N) % WIDE
    good = index < ROWS
    source = np.where(good, ROWS * device + index, 0)
    fy = np.where(good[:, None], forward[source], 0.0)
    iy = np.where(good[None, :], inverse[:, source], 0.0)
    ix = np.zeros((W, N))
    ix[:, :I] = inverse
    ix = np.stack([pair(ix[: W // 2]), pair(ix[W // 2 :])])
    magnitude = np.minimum(waves, N - waves)
    lap = 4.0 * np.sin(np.pi * waves / N) ** 2
    line = np.zeros((8, W), np.float32)
    line[0], line[1] = lap, magnitude
    return pair(fx), pair(fy), pair(iy), ix, line


def split(value):
    high = value.astype(BF16)
    return high, (value - high.astype(F32)).astype(BF16)


def total(product, rows):
    return (
        (product[rows:, 128:] + product[:rows, 128:]) + product[rows:, :128]
    ) + product[:rows, :128]


def split_three(value):
    high, rest = value.astype(BF16), value
    rest = rest - high.astype(F32)
    middle = rest.astype(BF16)
    return high, middle, (rest - middle.astype(F32)).astype(BF16)


def kernel(
    x_hbm, to_hbm, from_hbm, depth_hbm, line_hbm, fx_hbm, fy_hbm, iy_hbm, ix_hbm, out_hbm,
    x_ref, to_ref, from_ref, depth_ref, line_ref, out_ref, fx, fy, iy, ix, xf, xs, ys, qs, ms, zs, part,
    swap_x, spec_x, send_a, recv_a, mid_a, mid_b, send_b, recv_b, home, other,
    in_sem, out_sem, fx_sem, table_sem, swap_sem, s1_sem, s2_sem, r2_sem, s3_sem, r3_sem, all_sem,
):
    wide = lax.axis_index("wide")
    lev = lax.axis_index("lev")
    core = lev & 1
    half = lev >> 1
    ring = wide & (RING - 1)
    me = half * WIDE + wide
    partner = {"wide": wide, "lev": lev ^ 1}

    def chip(s):
        return {"wide": s & (WIDE - 1), "lev": ((s >> 6) << 1) + core}

    def across(q):
        return chip((q << 3) + ring)

    cross = me >> 3

    small = [
        pltpu.make_async_copy(source, target, in_sem.at[n])
        for n, (source, target) in enumerate(
            (
                (x_hbm, x_ref), (to_hbm, to_ref), (from_hbm, from_ref),
                (depth_hbm, depth_ref), (line_hbm, line_ref),
            )
        )
    ]
    small[0].start()

    blocks = [(core ^ 1) * COLS + c for c in range(COLS)] + [core * COLS + c for c in range(COLS)]
    fx_copies = []
    for n, block in enumerate(blocks):
        copy = pltpu.make_async_copy(fx_hbm.at[block], fx.at[n], fx_sem.at[n])
        copy.start()
        fx_copies.append(copy)
    rest = [
        pltpu.make_async_copy(source, target, table_sem.at[n])
        for n, (source, target) in enumerate(((fy_hbm, fy), (iy_hbm, iy), (ix_hbm, ix)))
    ]

    barrier = pltpu.get_barrier_semaphore()
    for step in range(1, RING):
        z = (ring + step) & (RING - 1)
        pl.semaphore_signal(
            barrier, inc=1, device_id=chip(me - ring + z), device_id_type=MESH
        )
    for step in range(1, 16):
        pl.semaphore_signal(
            barrier, inc=1, device_id=across((cross + step) & 15), device_id_type=MESH
        )
    pl.semaphore_signal(barrier, inc=1, device_id=partner, device_id_type=MESH)

    xf[...] = jnp.zeros_like(xf)
    small[0].wait()
    for l in range(LOC):
        xf[l * PAD : l * PAD + ROWS, :I] = x_ref[l]
    high, low = split(xf[...])
    xs[:80] = high
    xs[80:] = low

    def swap_copy(c):
        return pltpu.make_async_remote_copy(
            src_ref=swap_x.at[c],
            dst_ref=spec_x.at[pl.ds(core * LOC, LOC), c],
            send_sem=s1_sem,
            recv_sem=swap_sem,
            device_id=partner,
            device_id_type=MESH,
        )

    for n in range(2 * COLS):
        fx_copies[n].wait()
        block = total(jnp.dot(xs[...], fx[n], preferred_element_type=F32), 80)[: LOC * PAD]
        block = block.reshape(LOC, PAD, 128)
        if n < COLS:
            swap_x[n] = block
            if n == COLS - 1:
                pl.semaphore_wait(barrier, RING - 1 + 15 + 1)
                for c in range(COLS):
                    swap_copy(c).start()
                for step in range(1, 16):
                    pl.semaphore_signal(
                        all_sem, inc=1, device_id=across((cross + step) & 15), device_id_type=MESH
                    )
        else:
            for l in range(LOC):
                spec_x[core * LOC + l, n - COLS] = block[l]

    for copy in small[1:] + rest:
        copy.start()

    def bulk(ref, sem):
        return pltpu.make_async_copy(ref, ref, sem)

    bulk(spec_x.at[pl.ds(0, LOC)], swap_sem).wait()

    def pack(rows, buffer):
        last = rows(LAST)
        for l in range(LAST):
            tail = last[32 * l : 32 * l + 32] if l < 3 else jnp.zeros((32, 128), F32)
            buffer[pl.ds(l, CHIPS, stride=8), :] = jnp.concatenate([rows(l), tail], axis=0).T

    def unpack(buffer, store):
        for l in range(LAST):
            rows = buffer[pl.ds(l, CHIPS, stride=8), :].T
            store(l, 0, rows[:96])
            if l < 3:
                store(LAST, 32 * l, rows[96:])

    pack(lambda l: spec_x[l].reshape(96, 128), send_a)

    def exchange(source, target, send_sem, recv_sem, between=None):
        def copy(s):
            return pltpu.make_async_remote_copy(
                src_ref=source.at[pl.ds(pl.multiple_of(s * 8, 8), LAST)],
                dst_ref=target.at[pl.ds(pl.multiple_of(me * 8, 8), LAST)],
                send_sem=send_sem,
                recv_sem=recv_sem,
                device_id=chip(s),
                device_id_type=MESH,
            )

        for step in range(1, RING):
            copy(me - ring + ((ring + step) & (RING - 1))).start()
        for step in range(1, 16):
            copy((((cross + step) & 15) << 3) + ring).start()
        if between is not None:
            between()

        @pl.loop(1, 16)
        def _(step):
            q = ((cross + step) & 15) << 3
            for turn in range(1, RING):
                copy(q + ((ring + turn) & (RING - 1))).start()

        own = pl.ds(pl.multiple_of(me * 8, 8), 8)
        target[own, :] = source[own, :]

    def arrived(buffer, sem):
        bulk(buffer.at[pl.ds(0, (CHIPS - 1) * LAST)], sem).wait()

    exchange(
        send_a, recv_a, s2_sem, r2_sem, between=lambda: pl.semaphore_wait(all_sem, 15)
    )

    row = lax.broadcasted_iota(jnp.int32, (M, 1), 0)
    pick = ((row >> 2) == lax.broadcasted_iota(jnp.int32, (M, K), 1)).astype(F32)
    turn = lax.broadcasted_iota(jnp.int32, (6 * M, 1), 0)
    turn = lax.rem(turn, M) >> 2
    pick_six = (turn == lax.broadcasted_iota(jnp.int32, (6 * M, K), 1)).astype(F32)
    lane = lax.broadcasted_iota(jnp.int32, (M, 6 * M), 1)
    same = (row & 3) == (lane & 3)

    def expand(small):
        tall = jnp.dot(pick, small, preferred_element_type=F32, precision=lax.Precision.HIGHEST)
        full = lax.dot_general(
            tall, pick_six, (((1,), (1,)), ((), ())),
            preferred_element_type=F32, precision=lax.Precision.HIGHEST,
        )
        full = jnp.where(same, full, 0.0)
        high = full.astype(BF16).astype(F32)
        middle = (full - high).astype(BF16).astype(F32)
        low = full - high - middle
        return jnp.where(lane < 3 * M, high, jnp.where(lane < 5 * M, middle, low)).astype(BF16)

    for copy in small[1:]:
        copy.wait()
    to_big = expand(to_ref[...])
    from_big = expand(from_ref[...])
    depth = jnp.sum(pick * depth_ref[...], axis=1, keepdims=True)
    column = core * (W // 2) + (row & 3) * CHIPS + me
    hit = lax.broadcasted_iota(jnp.int32, (M, W), 1) == column
    lap_q = jnp.sum(jnp.where(hit, line_ref[0:1], 0.0), axis=1, keepdims=True)
    mag_q = jnp.sum(jnp.where(hit, line_ref[1:2], 0.0), axis=1, keepdims=True)
    left = lax.broadcasted_iota(jnp.int32, (M // 2, 128), 1) < WIDE

    def triple(value, lanes):
        high, middle, low = split_three(value)
        for n, piece in enumerate((high, middle, low, high, middle, high)):
            qs[n * M : (n + 1) * M, lanes] = piece

    arrived(recv_a, r2_sem)

    def store_a(l, at, rows):
        mid_a[l * 96 + at : l * 96 + at + rows.shape[0]] = rows

    unpack(recv_a, store_a)
    for t in range(PAD // 2):
        a = mid_a[pl.ds(2 * t, M // 2, stride=PAD), :]
        b = mid_a[pl.ds(2 * t + 1, M // 2, stride=PAD), :]
        first = jnp.where(left, a, pltpu.roll(b, WIDE, 1))
        second = jnp.where(left, pltpu.roll(a, WIDE, 1), b)
        high, low = split(jnp.concatenate([first, second], axis=0))
        ys[:M, t * 128 : t * 128 + 128] = high
        ys[M:, t * 128 : t * 128 + 128] = low

    rest[0].wait()

    for j in range(W // 128):
        lanes = slice(j * 128, j * 128 + 128)
        triple(total(jnp.dot(ys[...], fy[j], preferred_element_type=F32), M), lanes)
    lap_p = line_ref[0:1]
    mag_p = line_ref[1:2]
    keep = (mag_p * mag_p + mag_q * mag_q < float(KT * KT)).astype(F32)
    modes = jnp.dot(to_big, qs[...], preferred_element_type=F32)
    triple(modes * keep / (1.0 + depth * (lap_p + lap_q)), slice(0, W))
    high, low = split(jnp.dot(from_big, qs[...], preferred_element_type=F32))
    ms[:M] = high
    ms[M:] = low

    rest[1].wait()
    for t in range(PAD // 2):
        value = total(jnp.dot(ms[...], iy[t], preferred_element_type=F32), M)
        first, second = value[: M // 2], value[M // 2 :]
        mid_b[pl.ds(2 * t, M // 2, stride=PAD), :] = jnp.where(
            left, first, pltpu.roll(second, WIDE, 1)
        )
        mid_b[pl.ds(2 * t + 1, M // 2, stride=PAD), :] = jnp.where(
            left, pltpu.roll(first, WIDE, 1), second
        )
    pack(lambda l: mid_b[l * 96 : l * 96 + 96], send_b)
    exchange(send_b, recv_b, s3_sem, r3_sem)
    rest[2].wait()
    arrived(recv_b, r3_sem)

    def store_b(l, at, rows):
        home[l, at : at + rows.shape[0]] = rows

    unpack(recv_b, store_b)
    back = pltpu.make_async_remote_copy(
        src_ref=home.at[pl.ds((core ^ 1) * LOC, LOC)],
        dst_ref=other,
        send_sem=table_sem.at[3],
        recv_sem=table_sem.at[4],
        device_id=partner,
        device_id_type=MESH,
    )
    back.start()

    def gather(level):
        for c in range(COLS):
            rows = [level(l)[PAD * c : PAD * c + PAD] for l in range(LOC)]
            high, low = split(jnp.concatenate(rows + [jnp.zeros((8, 128), F32)], axis=0))
            zs[:80, c * 128 : c * 128 + 128] = high
            zs[80:, c * 128 : c * 128 + 128] = low

    gather(lambda l: home[core * LOC + l])
    for j in range(N // 128):
        part[:, j * 128 : j * 128 + 128] = total(
            jnp.dot(zs[...], ix[core, j], preferred_element_type=F32), 80
        )
    back.wait_recv()
    gather(lambda l: other[l])
    leaving = []
    for j in range(N // 128):
        field = total(jnp.dot(zs[...], ix[core ^ 1, j], preferred_element_type=F32), 80)
        field = field + part[:, j * 128 : j * 128 + 128]
        width = min(128, I - j * 128)
        for l in range(LOC):
            out_ref[l, :, j * 128 : j * 128 + width] = field[l * PAD : l * PAD + ROWS, :width]
        if j % 3 == 2:
            lanes = slice((j - 2) * 128, j * 128 + width)
            copy = pltpu.make_async_copy(
                out_ref.at[:, :, lanes], out_hbm.at[:, :, lanes], out_sem.at[j // 3]
            )
            copy.start()
            leaving.append(copy)

    for copy in leaving:
        copy.wait()
    bulk(swap_x, s1_sem).wait()
    arrived(send_a, s2_sem)
    arrived(send_b, s3_sem)
    back.wait_send()


def shards(state_field, to_modes, from_modes, mode_depth):
    fx, fy, iy, ix, line = (jnp.asarray(table) for table in tables())
    hbm = pl.BlockSpec(memory_space=pl.ANY)
    dma = pltpu.SemaphoreType.DMA
    return pl.pallas_call(
        kernel,
        out_shape=jax.ShapeDtypeStruct((LOC, ROWS, I), F32),
        in_specs=[hbm] * 9,
        out_specs=hbm,
        scratch_shapes=[
            pltpu.VMEM((LOC, ROWS, I), F32),
            pltpu.VMEM((K, K), F32),
            pltpu.VMEM((K, K), F32),
            pltpu.VMEM((1, K), F32),
            pltpu.VMEM(line.shape, F32),
            pltpu.VMEM((LOC, ROWS, I), F32),
            pltpu.VMEM(fx.shape, BF16),
            pltpu.VMEM(fy.shape, BF16),
            pltpu.VMEM(iy.shape, BF16),
            pltpu.VMEM(ix.shape, BF16),
            pltpu.VMEM((80, N), F32),
            pltpu.VMEM((160, N), BF16),
            pltpu.VMEM((2 * M, N), BF16),
            pltpu.VMEM((6 * M, W), BF16),
            pltpu.VMEM((2 * M, W), BF16),
            pltpu.VMEM((160, W // 2), BF16),
            pltpu.VMEM((80, N), F32),
            pltpu.VMEM((COLS, LOC, PAD, 128), F32),
            pltpu.VMEM((2 * LOC, COLS, PAD, 128), F32),
            pltpu.VMEM((8 * CHIPS, 128), F32),
            pltpu.VMEM((8 * CHIPS, 128), F32),
            pltpu.VMEM((2 * LOC * 96, 128), F32),
            pltpu.VMEM((2 * LOC * 96, 128), F32),
            pltpu.VMEM((8 * CHIPS, 128), F32),
            pltpu.VMEM((8 * CHIPS, 128), F32),
            pltpu.VMEM((2 * LOC, 96, 128), F32),
            pltpu.VMEM((LOC, 96, 128), F32),
            dma((5,)),
            dma((4,)),
            dma((2 * COLS,)),
            dma((5,)),
            dma,
            dma,
            dma,
            dma,
            dma,
            dma,
            pltpu.SemaphoreType.REGULAR,
        ],
        compiler_params=pltpu.CompilerParams(
            collective_id=0, has_side_effects=True, vmem_limit_bytes=56 * 2**20
        ),
        cost_estimate=pl.CostEstimate(flops=4 * 10**9, bytes_accessed=27 * 10**6, transcendentals=0),
    )(state_field, to_modes, from_modes, mode_depth.reshape(1, K), line, fx, fy, iy, ix)


def solution(mesh):
    assert dict(mesh.shape) == {"wide": WIDE, "lev": LEV}
    placed = (P("lev", "wide", None), P(), P(), P())
    return jax.shard_map(
        shards, mesh=mesh, in_specs=placed, out_specs=P("lev", "wide", None), check_vma=False
    )
```

```python
import functools
import math

import jax
import jax.numpy as jnp
import ml_dtypes
import numpy as np
from jax import lax
from jax.experimental import pallas as pl
from jax.experimental.pallas import tpu as pltpu
from jax.sharding import PartitionSpec as P

I = 1472
E = 64
K = 12
KT = 512
N = I + E
W = 2 * KT
RING = 8
WIDE = 64
LEV = 4
CHIPS = 128
LOC = 3
ROWS = 23
PAD = 24
COLS = 4
LAST = 5
M = K * COLS
MESH = pl.DeviceIdType.MESH
F32 = jnp.float32
BF16 = jnp.bfloat16


def wave_of(position):
    return np.where(position < KT, position, position + N - W)


def pair(table):
    high = table.astype(ml_dtypes.bfloat16)
    low = (table - high.astype(np.float64)).astype(ml_dtypes.bfloat16)
    depth, width = table.shape
    blocks = width // 128
    both = np.stack([high.reshape(depth, blocks, 128), low.reshape(depth, blocks, 128)], axis=2)
    return np.ascontiguousarray(both.transpose(1, 0, 2, 3).reshape(blocks, depth, 256))


@functools.lru_cache(maxsize=None)
def tables():
    position = np.arange(W)
    waves = wave_of(position)
    angle = 2.0 * np.pi / N * ((np.arange(N)[:, None] * waves[None, :]) % N)
    cas = np.cos(angle) + np.sin(angle)
    f = (np.arange(E) + 1.0) / (E + 1.0)
    h00, h10 = 2 * f**3 - 3 * f**2 + 1, f**3 - 2 * f**2 + f
    h01, h11 = -2 * f**3 + 3 * f**2, f**3 - f**2
    forward = cas[:I].copy()
    forward[I - 1] += (h00 + h10) @ cas[I:]
    forward[I - 2] -= h10 @ cas[I:]
    forward[0] += (h01 - h11) @ cas[I:]
    forward[1] += h11 @ cas[I:]
    inverse = cas[:I].T / N

    fx = np.zeros((N, W))
    fx[:I] = forward
    index, device = np.arange(N) // WIDE, np.arange(N) % WIDE
    good = index < ROWS
    source = np.where(good, ROWS * device + index, 0)
    fy = np.where(good[:, None], forward[source], 0.0)
    iy = np.where(good[None, :], inverse[:, source], 0.0)
    ix = np.zeros((W, N))
    ix[:, :I] = inverse
    ix = np.stack([pair(ix[: W // 2]), pair(ix[W // 2 :])])
    magnitude = np.minimum(waves, N - waves)
    lap = 4.0 * np.sin(np.pi * waves / N) ** 2
    line = np.zeros((8, W), np.float32)
    line[0], line[1] = lap, magnitude
    return pair(fx), pair(fy), pair(iy), ix, line


def split(value):
    high = value.astype(BF16)
    return high, (value - high.astype(F32)).astype(BF16)


def total(product, rows):
    return (
        (product[rows:, 128:] + product[:rows, 128:]) + product[rows:, :128]
    ) + product[:rows, :128]


def split_three(value):
    high, rest = value.astype(BF16), value
    rest = rest - high.astype(F32)
    middle = rest.astype(BF16)
    return high, middle, (rest - middle.astype(F32)).astype(BF16)


def kernel(
    x_hbm, to_hbm, from_hbm, depth_hbm, line_hbm, fx_hbm, fy_hbm, iy_hbm, ix_hbm, out_ref,
    x_ref, to_ref, from_ref, depth_ref, line_ref, fx, fy, iy, ix, xf, xs, ys, qs, ms, zs, part,
    swap_x, spec_x, send_a, recv_a, mid_a, mid_b, send_b, recv_b, home, other,
    in_sem, fx_sem, table_sem, swap_sem, s1_sem, s2_sem, r2_sem, s3_sem, r3_sem, all_sem,
):
    wide = lax.axis_index("wide")
    lev = lax.axis_index("lev")
    core = lev & 1
    half = lev >> 1
    ring = wide & (RING - 1)
    me = half * WIDE + wide
    partner = {"wide": wide, "lev": lev ^ 1}

    def chip(s):
        return {"wide": s & (WIDE - 1), "lev": ((s >> 6) << 1) + core}

    def across(q):
        return chip((q << 3) + ring)

    cross = me >> 3

    small = [
        pltpu.make_async_copy(source, target, in_sem.at[n])
        for n, (source, target) in enumerate(
            (
                (x_hbm, x_ref), (to_hbm, to_ref), (from_hbm, from_ref),
                (depth_hbm, depth_ref), (line_hbm, line_ref),
            )
        )
    ]
    small[0].start()

    blocks = [(core ^ 1) * COLS + c for c in range(COLS)] + [core * COLS + c for c in range(COLS)]
    fx_copies = []
    for n, block in enumerate(blocks):
        copy = pltpu.make_async_copy(fx_hbm.at[block], fx.at[n], fx_sem.at[n])
        copy.start()
        fx_copies.append(copy)
    rest = [
        pltpu.make_async_copy(source, target, table_sem.at[n])
        for n, (source, target) in enumerate(((fy_hbm, fy), (iy_hbm, iy), (ix_hbm, ix)))
    ]

    barrier = pltpu.get_barrier_semaphore()
    for step in range(1, RING):
        z = (ring + step) & (RING - 1)
        pl.semaphore_signal(
            barrier, inc=1, device_id=chip(me - ring + z), device_id_type=MESH
        )
    for step in range(1, 16):
        pl.semaphore_signal(
            barrier, inc=1, device_id=across((cross + step) & 15), device_id_type=MESH
        )
    pl.semaphore_signal(barrier, inc=1, device_id=partner, device_id_type=MESH)

    xf[...] = jnp.zeros_like(xf)
    small[0].wait()
    for l in range(LOC):
        xf[l * PAD : l * PAD + ROWS, :I] = x_ref[l]
    high, low = split(xf[...])
    xs[:80] = high
    xs[80:] = low

    def swap_copy(c):
        return pltpu.make_async_remote_copy(
            src_ref=swap_x.at[c],
            dst_ref=spec_x.at[pl.ds(core * LOC, LOC), c],
            send_sem=s1_sem,
            recv_sem=swap_sem,
            device_id=partner,
            device_id_type=MESH,
        )

    for n in range(2 * COLS):
        fx_copies[n].wait()
        block = total(jnp.dot(xs[...], fx[n], preferred_element_type=F32), 80)[: LOC * PAD]
        block = block.reshape(LOC, PAD, 128)
        if n < COLS:
            swap_x[n] = block
            if n == COLS - 1:
                pl.semaphore_wait(barrier, RING - 1 + 15 + 1)
                for c in range(COLS):
                    swap_copy(c).start()
                for step in range(1, 16):
                    pl.semaphore_signal(
                        all_sem, inc=1, device_id=across((cross + step) & 15), device_id_type=MESH
                    )
        else:
            for l in range(LOC):
                spec_x[core * LOC + l, n - COLS] = block[l]

    for copy in small[1:] + rest:
        copy.start()

    def bulk(ref, sem):
        return pltpu.make_async_copy(ref, ref, sem)

    bulk(spec_x.at[pl.ds(0, LOC)], swap_sem).wait()

    def pack(rows, buffer):
        last = rows(LAST)
        for l in range(LAST):
            tail = last[32 * l : 32 * l + 32] if l < 3 else jnp.zeros((32, 128), F32)
            buffer[pl.ds(l, CHIPS, stride=8), :] = jnp.concatenate([rows(l), tail], axis=0).T

    def unpack(buffer, store):
        for l in range(LAST):
            rows = buffer[pl.ds(l, CHIPS, stride=8), :].T
            store(l, 0, rows[:96])
            if l < 3:
                store(LAST, 32 * l, rows[96:])

    pack(lambda l: spec_x[l].reshape(96, 128), send_a)

    def exchange(source, target, send_sem, recv_sem, between=None):
        def copy(s):
            return pltpu.make_async_remote_copy(
                src_ref=source.at[pl.ds(pl.multiple_of(s * 8, 8), LAST)],
                dst_ref=target.at[pl.ds(pl.multiple_of(me * 8, 8), LAST)],
                send_sem=send_sem,
                recv_sem=recv_sem,
                device_id=chip(s),
                device_id_type=MESH,
            )

        for step in range(1, RING):
            copy(me - ring + ((ring + step) & (RING - 1))).start()
        for step in range(1, 16):
            copy((((cross + step) & 15) << 3) + ring).start()
        if between is not None:
            between()

        @pl.loop(1, 16)
        def _(step):
            q = ((cross + step) & 15) << 3
            for turn in range(1, RING):
                copy(q + ((ring + turn) & (RING - 1))).start()

        own = pl.ds(pl.multiple_of(me * 8, 8), 8)
        target[own, :] = source[own, :]

    def arrived(buffer, sem):
        bulk(buffer.at[pl.ds(0, (CHIPS - 1) * LAST)], sem).wait()

    exchange(
        send_a, recv_a, s2_sem, r2_sem, between=lambda: pl.semaphore_wait(all_sem, 15)
    )

    row = lax.broadcasted_iota(jnp.int32, (M, 1), 0)
    pick = ((row >> 2) == lax.broadcasted_iota(jnp.int32, (M, K), 1)).astype(F32)
    turn = lax.broadcasted_iota(jnp.int32, (6 * M, 1), 0)
    turn = lax.rem(turn, M) >> 2
    pick_six = (turn == lax.broadcasted_iota(jnp.int32, (6 * M, K), 1)).astype(F32)
    lane = lax.broadcasted_iota(jnp.int32, (M, 6 * M), 1)
    same = (row & 3) == (lane & 3)

    def expand(small):
        tall = jnp.dot(pick, small, preferred_element_type=F32, precision=lax.Precision.HIGHEST)
        full = lax.dot_general(
            tall, pick_six, (((1,), (1,)), ((), ())),
            preferred_element_type=F32, precision=lax.Precision.HIGHEST,
        )
        full = jnp.where(same, full, 0.0)
        high = full.astype(BF16).astype(F32)
        middle = (full - high).astype(BF16).astype(F32)
        low = full - high - middle
        return jnp.where(lane < 3 * M, high, jnp.where(lane < 5 * M, middle, low)).astype(BF16)

    for copy in small[1:]:
        copy.wait()
    to_big = expand(to_ref[...])
    from_big = expand(from_ref[...])
    depth = jnp.sum(pick * depth_ref[...], axis=1, keepdims=True)
    column = core * (W // 2) + (row & 3) * CHIPS + me
    hit = lax.broadcasted_iota(jnp.int32, (M, W), 1) == column
    lap_q = jnp.sum(jnp.where(hit, line_ref[0:1], 0.0), axis=1, keepdims=True)
    mag_q = jnp.sum(jnp.where(hit, line_ref[1:2], 0.0), axis=1, keepdims=True)
    left = lax.broadcasted_iota(jnp.int32, (M // 2, 128), 1) < WIDE

    def triple(value, lanes):
        high, middle, low = split_three(value)
        for n, piece in enumerate((high, middle, low, high, middle, high)):
            qs[n * M : (n + 1) * M, lanes] = piece

    arrived(recv_a, r2_sem)

    def store_a(l, at, rows):
        mid_a[l * 96 + at : l * 96 + at + rows.shape[0]] = rows

    unpack(recv_a, store_a)
    for t in range(PAD // 2):
        a = mid_a[pl.ds(2 * t, M // 2, stride=PAD), :]
        b = mid_a[pl.ds(2 * t + 1, M // 2, stride=PAD), :]
        first = jnp.where(left, a, pltpu.roll(b, WIDE, 1))
        second = jnp.where(left, pltpu.roll(a, WIDE, 1), b)
        high, low = split(jnp.concatenate([first, second], axis=0))
        ys[:M, t * 128 : t * 128 + 128] = high
        ys[M:, t * 128 : t * 128 + 128] = low

    rest[0].wait()

    for j in range(W // 128):
        lanes = slice(j * 128, j * 128 + 128)
        triple(total(jnp.dot(ys[...], fy[j], preferred_element_type=F32), M), lanes)
    lap_p = line_ref[0:1]
    mag_p = line_ref[1:2]
    keep = (mag_p * mag_p + mag_q * mag_q < float(KT * KT)).astype(F32)
    modes = jnp.dot(to_big, qs[...], preferred_element_type=F32)
    triple(modes * keep / (1.0 + depth * (lap_p + lap_q)), slice(0, W))
    high, low = split(jnp.dot(from_big, qs[...], preferred_element_type=F32))
    ms[:M] = high
    ms[M:] = low

    rest[1].wait()
    for t in range(PAD // 2):
        value = total(jnp.dot(ms[...], iy[t], preferred_element_type=F32), M)
        first, second = value[: M // 2], value[M // 2 :]
        mid_b[pl.ds(2 * t, M // 2, stride=PAD), :] = jnp.where(
            left, first, pltpu.roll(second, WIDE, 1)
        )
        mid_b[pl.ds(2 * t + 1, M // 2, stride=PAD), :] = jnp.where(
            left, pltpu.roll(first, WIDE, 1), second
        )
    pack(lambda l: mid_b[l * 96 : l * 96 + 96], send_b)
    exchange(send_b, recv_b, s3_sem, r3_sem)
    rest[2].wait()
    arrived(recv_b, r3_sem)

    def store_b(l, at, rows):
        home[l, at : at + rows.shape[0]] = rows

    unpack(recv_b, store_b)
    back = pltpu.make_async_remote_copy(
        src_ref=home.at[pl.ds((core ^ 1) * LOC, LOC)],
        dst_ref=other,
        send_sem=table_sem.at[3],
        recv_sem=table_sem.at[4],
        device_id=partner,
        device_id_type=MESH,
    )
    back.start()

    def gather(level):
        for c in range(COLS):
            rows = [level(l)[PAD * c : PAD * c + PAD] for l in range(LOC)]
            high, low = split(jnp.concatenate(rows + [jnp.zeros((8, 128), F32)], axis=0))
            zs[:80, c * 128 : c * 128 + 128] = high
            zs[80:, c * 128 : c * 128 + 128] = low

    gather(lambda l: home[core * LOC + l])
    for j in range(N // 128):
        part[:, j * 128 : j * 128 + 128] = total(
            jnp.dot(zs[...], ix[core, j], preferred_element_type=F32), 80
        )
    back.wait_recv()
    gather(lambda l: other[l])
    for j in range(N // 128):
        field = total(jnp.dot(zs[...], ix[core ^ 1, j], preferred_element_type=F32), 80)
        field = field + part[:, j * 128 : j * 128 + 128]
        width = min(128, I - j * 128)
        for l in range(LOC):
            out_ref[l, :, j * 128 : j * 128 + width] = field[l * PAD : l * PAD + ROWS, :width]

    bulk(swap_x, s1_sem).wait()
    arrived(send_a, s2_sem)
    arrived(send_b, s3_sem)
    back.wait_send()


def shards(state_field, to_modes, from_modes, mode_depth):
    fx, fy, iy, ix, line = (jnp.asarray(table) for table in tables())
    hbm = pl.BlockSpec(memory_space=pl.ANY)
    dma = pltpu.SemaphoreType.DMA
    return pl.pallas_call(
        kernel,
        out_shape=pltpu.VMEM((LOC, ROWS, I), F32),
        in_specs=[hbm] * 9,
        out_specs=pl.BlockSpec(memory_space=pltpu.VMEM),
        scratch_shapes=[
            pltpu.VMEM((LOC, ROWS, I), F32),
            pltpu.VMEM((K, K), F32),
            pltpu.VMEM((K, K), F32),
            pltpu.VMEM((1, K), F32),
            pltpu.VMEM(line.shape, F32),
            pltpu.VMEM(fx.shape, BF16),
            pltpu.VMEM(fy.shape, BF16),
            pltpu.VMEM(iy.shape, BF16),
            pltpu.VMEM(ix.shape, BF16),
            pltpu.VMEM((80, N), F32),
            pltpu.VMEM((160, N), BF16),
            pltpu.VMEM((2 * M, N), BF16),
            pltpu.VMEM((6 * M, W), BF16),
            pltpu.VMEM((2 * M, W), BF16),
            pltpu.VMEM((160, W // 2), BF16),
            pltpu.VMEM((80, N), F32),
            pltpu.VMEM((COLS, LOC, PAD, 128), F32),
            pltpu.VMEM((2 * LOC, COLS, PAD, 128), F32),
            pltpu.VMEM((8 * CHIPS, 128), F32),
            pltpu.VMEM((8 * CHIPS, 128), F32),
            pltpu.VMEM((2 * LOC * 96, 128), F32),
            pltpu.VMEM((2 * LOC * 96, 128), F32),
            pltpu.VMEM((8 * CHIPS, 128), F32),
            pltpu.VMEM((8 * CHIPS, 128), F32),
            pltpu.VMEM((2 * LOC, 96, 128), F32),
            pltpu.VMEM((LOC, 96, 128), F32),
            dma((5,)),
            dma((2 * COLS,)),
            dma((5,)),
            dma,
            dma,
            dma,
            dma,
            dma,
            dma,
            pltpu.SemaphoreType.REGULAR,
        ],
        compiler_params=pltpu.CompilerParams(
            collective_id=0, has_side_effects=True, vmem_limit_bytes=56 * 2**20
        ),
        cost_estimate=pl.CostEstimate(flops=4 * 10**9, bytes_accessed=27 * 10**6, transcendentals=0),
    )(state_field, to_modes, from_modes, mode_depth.reshape(1, K), line, fx, fy, iy, ix)


def solution(mesh):
    assert dict(mesh.shape) == {"wide": WIDE, "lev": LEV}
    placed = (P("lev", "wide", None), P(), P(), P())
    return jax.shard_map(
        shards, mesh=mesh, in_specs=placed, out_specs=P("lev", "wide", None), check_vma=False
    )
```

```python
import functools
import math

import jax
import jax.numpy as jnp
import ml_dtypes
import numpy as np
from jax import lax
from jax.experimental import pallas as pl
from jax.experimental.pallas import tpu as pltpu
from jax.sharding import PartitionSpec as P

I = 1472
E = 64
K = 12
KT = 512
N = I + E
W = 2 * KT
RING = 8
WIDE = 64
LEV = 4
CHIPS = 128
LOC = 3
ROWS = 23
PAD = 24
COLS = 4
LAST = 5
M = K * COLS
MESH = pl.DeviceIdType.MESH
F32 = jnp.float32
BF16 = jnp.bfloat16


def wave_of(position):
    return np.where(position < KT, position, position + N - W)


def pair(table):
    high = table.astype(ml_dtypes.bfloat16)
    low = (table - high.astype(np.float64)).astype(ml_dtypes.bfloat16)
    depth, width = table.shape
    blocks = width // 128
    both = np.stack([high.reshape(depth, blocks, 128), low.reshape(depth, blocks, 128)], axis=2)
    return np.ascontiguousarray(both.transpose(1, 0, 2, 3).reshape(blocks, depth, 256))


@functools.lru_cache(maxsize=None)
def tables():
    position = np.arange(W)
    waves = wave_of(position)
    angle = 2.0 * np.pi / N * ((np.arange(N)[:, None] * waves[None, :]) % N)
    cas = np.cos(angle) + np.sin(angle)
    f = (np.arange(E) + 1.0) / (E + 1.0)
    h00, h10 = 2 * f**3 - 3 * f**2 + 1, f**3 - 2 * f**2 + f
    h01, h11 = -2 * f**3 + 3 * f**2, f**3 - f**2
    forward = cas[:I].copy()
    forward[I - 1] += (h00 + h10) @ cas[I:]
    forward[I - 2] -= h10 @ cas[I:]
    forward[0] += (h01 - h11) @ cas[I:]
    forward[1] += h11 @ cas[I:]
    inverse = cas[:I].T / N

    fx = np.zeros((N, W))
    fx[:I] = forward
    index, device = np.arange(N) // WIDE, np.arange(N) % WIDE
    good = index < ROWS
    source = np.where(good, ROWS * device + index, 0)
    fy = np.where(good[:, None], forward[source], 0.0)
    iy = np.where(good[None, :], inverse[:, source], 0.0)
    ix = np.zeros((W, N))
    ix[:, :I] = inverse
    ix = np.stack([pair(ix[: W // 2]), pair(ix[W // 2 :])])
    magnitude = np.minimum(waves, N - waves)
    lap = 4.0 * np.sin(np.pi * waves / N) ** 2
    line = np.zeros((8, W), np.float32)
    line[0], line[1] = lap, magnitude
    return pair(fx), pair(fy), pair(iy), ix, line


def split(value):
    high = value.astype(BF16)
    return high, (value - high.astype(F32)).astype(BF16)


def total(product, rows):
    return (
        (product[rows:, 128:] + product[:rows, 128:]) + product[rows:, :128]
    ) + product[:rows, :128]


def split_three(value):
    high, rest = value.astype(BF16), value
    rest = rest - high.astype(F32)
    middle = rest.astype(BF16)
    return high, middle, (rest - middle.astype(F32)).astype(BF16)


def kernel(
    x_hbm, to_hbm, from_hbm, depth_hbm, line_hbm, fx_hbm, fy_hbm, iy_hbm, ix_hbm, out_ref,
    x_ref, to_ref, from_ref, depth_ref, line_ref, fx, fy, iy, ix, xf, xs, ys, qs, ms, zs, part,
    swap_x, spec_x, send_a, recv_a, mid_a, mid_b, send_b, recv_b, home, other,
    in_sem, fx_sem, table_sem, swap_sem, s1_sem, s2_sem, r2_sem, s3_sem, r3_sem, all_sem,
):
    wide = lax.axis_index("wide")
    lev = lax.axis_index("lev")
    core = lev & 1
    half = lev >> 1
    ring = wide & (RING - 1)
    me = half * WIDE + wide
    partner = {"wide": wide, "lev": lev ^ 1}

    def chip(s):
        return {"wide": s & (WIDE - 1), "lev": ((s >> 6) << 1) + core}

    def across(q):
        return chip((q << 3) + ring)

    cross = me >> 3

    small = [
        pltpu.make_async_copy(source, target, in_sem.at[n])
        for n, (source, target) in enumerate(
            (
                (x_hbm, x_ref), (to_hbm, to_ref), (from_hbm, from_ref),
                (depth_hbm, depth_ref), (line_hbm, line_ref),
            )
        )
    ]
    small[0].start()

    blocks = [(core ^ 1) * COLS + c for c in range(COLS)] + [core * COLS + c for c in range(COLS)]
    fx_copies = []
    for n, block in enumerate(blocks):
        copy = pltpu.make_async_copy(fx_hbm.at[block], fx.at[n], fx_sem.at[n])
        copy.start()
        fx_copies.append(copy)
    rest = [
        pltpu.make_async_copy(source, target, table_sem.at[n])
        for n, (source, target) in enumerate(((fy_hbm, fy), (iy_hbm, iy), (ix_hbm, ix)))
    ]

    barrier = pltpu.get_barrier_semaphore()
    for step in range(1, RING):
        z = (ring + step) & (RING - 1)
        pl.semaphore_signal(
            barrier, inc=1, device_id=chip(me - ring + z), device_id_type=MESH
        )
    for step in range(1, 16):
        pl.semaphore_signal(
            barrier, inc=1, device_id=across((cross + step) & 15), device_id_type=MESH
        )
    pl.semaphore_signal(barrier, inc=1, device_id=partner, device_id_type=MESH)

    xf[...] = jnp.zeros_like(xf)
    small[0].wait()
    for l in range(LOC):
        xf[l * PAD : l * PAD + ROWS, :I] = x_ref[l]
    high, low = split(xf[...])
    xs[:80] = high
    xs[80:] = low

    def swap_copy(c):
        return pltpu.make_async_remote_copy(
            src_ref=swap_x.at[c],
            dst_ref=spec_x.at[pl.ds(core * LOC, LOC), c],
            send_sem=s1_sem,
            recv_sem=swap_sem,
            device_id=partner,
            device_id_type=MESH,
        )

    for n in range(2 * COLS):
        fx_copies[n].wait()
        block = total(jnp.dot(xs[...], fx[n], preferred_element_type=F32), 80)[: LOC * PAD]
        block = block.reshape(LOC, PAD, 128)
        if n < COLS:
            swap_x[n] = block
            if n == 0:
                pl.semaphore_wait(barrier, RING - 1 + 15 + 1)
                for step in range(1, 16):
                    pl.semaphore_signal(
                        all_sem, inc=1, device_id=across((cross + step) & 15), device_id_type=MESH
                    )
                for c in range(n):
                    swap_copy(c).start()
            if n >= 0:
                swap_copy(n).start()
        else:
            for l in range(LOC):
                spec_x[core * LOC + l, n - COLS] = block[l]

    for copy in small[1:] + rest:
        copy.start()

    def bulk(ref, sem):
        return pltpu.make_async_copy(ref, ref, sem)

    bulk(spec_x.at[pl.ds(0, LOC)], swap_sem).wait()

    def pack(rows, buffer):
        last = rows(LAST)
        for l in range(LAST):
            tail = last[32 * l : 32 * l + 32] if l < 3 else jnp.zeros((32, 128), F32)
            buffer[pl.ds(l, CHIPS, stride=8), :] = jnp.concatenate([rows(l), tail], axis=0).T

    def unpack(buffer, store):
        for l in range(LAST):
            rows = buffer[pl.ds(l, CHIPS, stride=8), :].T
            store(l, 0, rows[:96])
            if l < 3:
                store(LAST, 32 * l, rows[96:])

    pack(lambda l: spec_x[l].reshape(96, 128), send_a)

    def exchange(source, target, send_sem, recv_sem, between=None):
        def copy(s):
            return pltpu.make_async_remote_copy(
                src_ref=source.at[pl.ds(pl.multiple_of(s * 8, 8), LAST)],
                dst_ref=target.at[pl.ds(pl.multiple_of(me * 8, 8), LAST)],
                send_sem=send_sem,
                recv_sem=recv_sem,
                device_id=chip(s),
                device_id_type=MESH,
            )

        if between is not None:
            for step in range(1, RING):
                copy(me - ring + ((ring + step) & (RING - 1))).start()
            for step in range(1, 16):
                copy((((cross + step) & 15) << 3) + ring).start()
            between()

            @pl.loop(1, 16)
            def _(step):
                q = ((cross + step) & 15) << 3
                for turn in range(1, RING):
                    copy(q + ((ring + turn) & (RING - 1))).start()

        else:

            @pl.loop(1, CHIPS)
            def _(step):
                copy((me + step) & (CHIPS - 1)).start()

        own = pl.ds(pl.multiple_of(me * 8, 8), 8)
        target[own, :] = source[own, :]

    def arrived(buffer, sem):
        bulk(buffer.at[pl.ds(0, (CHIPS - 1) * LAST)], sem).wait()

    exchange(
        send_a, recv_a, s2_sem, r2_sem, between=lambda: pl.semaphore_wait(all_sem, 15)
    )

    row = lax.broadcasted_iota(jnp.int32, (M, 1), 0)
    pick = ((row >> 2) == lax.broadcasted_iota(jnp.int32, (M, K), 1)).astype(F32)
    turn = lax.broadcasted_iota(jnp.int32, (6 * M, 1), 0)
    turn = lax.rem(turn, M) >> 2
    pick_six = (turn == lax.broadcasted_iota(jnp.int32, (6 * M, K), 1)).astype(F32)
    lane = lax.broadcasted_iota(jnp.int32, (M, 6 * M), 1)
    same = (row & 3) == (lane & 3)

    def expand(small):
        tall = jnp.dot(pick, small, preferred_element_type=F32, precision=lax.Precision.HIGHEST)
        full = lax.dot_general(
            tall, pick_six, (((1,), (1,)), ((), ())),
            preferred_element_type=F32, precision=lax.Precision.HIGHEST,
        )
        full = jnp.where(same, full, 0.0)
        high = full.astype(BF16).astype(F32)
        middle = (full - high).astype(BF16).astype(F32)
        low = full - high - middle
        return jnp.where(lane < 3 * M, high, jnp.where(lane < 5 * M, middle, low)).astype(BF16)

    for copy in small[1:]:
        copy.wait()
    to_big = expand(to_ref[...])
    from_big = expand(from_ref[...])
    depth = jnp.sum(pick * depth_ref[...], axis=1, keepdims=True)
    column = core * (W // 2) + (row & 3) * CHIPS + me
    hit = lax.broadcasted_iota(jnp.int32, (M, W), 1) == column
    lap_q = jnp.sum(jnp.where(hit, line_ref[0:1], 0.0), axis=1, keepdims=True)
    mag_q = jnp.sum(jnp.where(hit, line_ref[1:2], 0.0), axis=1, keepdims=True)
    left = lax.broadcasted_iota(jnp.int32, (M // 2, 128), 1) < WIDE

    def triple(value, lanes):
        high, middle, low = split_three(value)
        for n, piece in enumerate((high, middle, low, high, middle, high)):
            qs[n * M : (n + 1) * M, lanes] = piece

    arrived(recv_a, r2_sem)

    def store_a(l, at, rows):
        mid_a[l * 96 + at : l * 96 + at + rows.shape[0]] = rows

    unpack(recv_a, store_a)
    for t in range(PAD // 2):
        a = mid_a[pl.ds(2 * t, M // 2, stride=PAD), :]
        b = mid_a[pl.ds(2 * t + 1, M // 2, stride=PAD), :]
        first = jnp.where(left, a, pltpu.roll(b, WIDE, 1))
        second = jnp.where(left, pltpu.roll(a, WIDE, 1), b)
        high, low = split(jnp.concatenate([first, second], axis=0))
        ys[:M, t * 128 : t * 128 + 128] = high
        ys[M:, t * 128 : t * 128 + 128] = low

    rest[0].wait()

    for j in range(W // 128):
        lanes = slice(j * 128, j * 128 + 128)
        triple(total(jnp.dot(ys[...], fy[j], preferred_element_type=F32), M), lanes)
    lap_p = line_ref[0:1]
    mag_p = line_ref[1:2]
    keep = (mag_p * mag_p + mag_q * mag_q < float(KT * KT)).astype(F32)
    modes = jnp.dot(to_big, qs[...], preferred_element_type=F32)
    triple(modes * keep / (1.0 + depth * (lap_p + lap_q)), slice(0, W))
    high, low = split(jnp.dot(from_big, qs[...], preferred_element_type=F32))
    ms[:M] = high
    ms[M:] = low

    rest[1].wait()
    for t in range(PAD // 2):
        value = total(jnp.dot(ms[...], iy[t], preferred_element_type=F32), M)
        first, second = value[: M // 2], value[M // 2 :]
        mid_b[pl.ds(2 * t, M // 2, stride=PAD), :] = jnp.where(
            left, first, pltpu.roll(second, WIDE, 1)
        )
        mid_b[pl.ds(2 * t + 1, M // 2, stride=PAD), :] = jnp.where(
            left, pltpu.roll(first, WIDE, 1), second
        )
    pack(lambda l: mid_b[l * 96 : l * 96 + 96], send_b)
    exchange(send_b, recv_b, s3_sem, r3_sem)
    rest[2].wait()
    arrived(recv_b, r3_sem)

    def store_b(l, at, rows):
        home[l, at : at + rows.shape[0]] = rows

    unpack(recv_b, store_b)
    back = pltpu.make_async_remote_copy(
        src_ref=home.at[pl.ds((core ^ 1) * LOC, LOC)],
        dst_ref=other,
        send_sem=table_sem.at[3],
        recv_sem=table_sem.at[4],
        device_id=partner,
        device_id_type=MESH,
    )
    back.start()

    def gather(level):
        for c in range(COLS):
            rows = [level(l)[PAD * c : PAD * c + PAD] for l in range(LOC)]
            high, low = split(jnp.concatenate(rows + [jnp.zeros((8, 128), F32)], axis=0))
            zs[:80, c * 128 : c * 128 + 128] = high
            zs[80:, c * 128 : c * 128 + 128] = low

    gather(lambda l: home[core * LOC + l])
    for j in range(N // 128):
        part[:, j * 128 : j * 128 + 128] = total(
            jnp.dot(zs[...], ix[core, j], preferred_element_type=F32), 80
        )
    back.wait_recv()
    gather(lambda l: other[l])
    for j in range(N // 128):
        field = total(jnp.dot(zs[...], ix[core ^ 1, j], preferred_element_type=F32), 80)
        field = field + part[:, j * 128 : j * 128 + 128]
        width = min(128, I - j * 128)
        for l in range(LOC):
            out_ref[l, :, j * 128 : j * 128 + width] = field[l * PAD : l * PAD + ROWS, :width]

    bulk(swap_x, s1_sem).wait()
    arrived(send_a, s2_sem)
    arrived(send_b, s3_sem)
    back.wait_send()


def shards(state_field, to_modes, from_modes, mode_depth):
    fx, fy, iy, ix, line = (jnp.asarray(table) for table in tables())
    hbm = pl.BlockSpec(memory_space=pl.ANY)
    dma = pltpu.SemaphoreType.DMA
    return pl.pallas_call(
        kernel,
        out_shape=pltpu.VMEM((LOC, ROWS, I), F32),
        in_specs=[hbm] * 9,
        out_specs=pl.BlockSpec(memory_space=pltpu.VMEM),
        scratch_shapes=[
            pltpu.VMEM((LOC, ROWS, I), F32),
            pltpu.VMEM((K, K), F32),
            pltpu.VMEM((K, K), F32),
            pltpu.VMEM((1, K), F32),
            pltpu.VMEM(line.shape, F32),
            pltpu.VMEM(fx.shape, BF16),
            pltpu.VMEM(fy.shape, BF16),
            pltpu.VMEM(iy.shape, BF16),
            pltpu.VMEM(ix.shape, BF16),
            pltpu.VMEM((80, N), F32),
            pltpu.VMEM((160, N), BF16),
            pltpu.VMEM((2 * M, N), BF16),
            pltpu.VMEM((6 * M, W), BF16),
            pltpu.VMEM((2 * M, W), BF16),
            pltpu.VMEM((160, W // 2), BF16),
            pltpu.VMEM((80, N), F32),
            pltpu.VMEM((COLS, LOC, PAD, 128), F32),
            pltpu.VMEM((2 * LOC, COLS, PAD, 128), F32),
            pltpu.VMEM((8 * CHIPS, 128), F32),
            pltpu.VMEM((8 * CHIPS, 128), F32),
            pltpu.VMEM((2 * LOC * 96, 128), F32),
            pltpu.VMEM((2 * LOC * 96, 128), F32),
            pltpu.VMEM((8 * CHIPS, 128), F32),
            pltpu.VMEM((8 * CHIPS, 128), F32),
            pltpu.VMEM((2 * LOC, 96, 128), F32),
            pltpu.VMEM((LOC, 96, 128), F32),
            dma((5,)),
            dma((2 * COLS,)),
            dma((5,)),
            dma,
            dma,
            dma,
            dma,
            dma,
            dma,
            pltpu.SemaphoreType.REGULAR,
        ],
        compiler_params=pltpu.CompilerParams(
            collective_id=0, has_side_effects=True, vmem_limit_bytes=56 * 2**20
        ),
        cost_estimate=pl.CostEstimate(flops=4 * 10**9, bytes_accessed=27 * 10**6, transcendentals=0),
    )(state_field, to_modes, from_modes, mode_depth.reshape(1, K), line, fx, fy, iy, ix)


def solution(mesh):
    assert dict(mesh.shape) == {"wide": WIDE, "lev": LEV}
    placed = (P("lev", "wide", None), P(), P(), P())
    return jax.shard_map(
        shards, mesh=mesh, in_specs=placed, out_specs=P("lev", "wide", None), check_vma=False
    )
```

```python
import functools
import math

import jax
import jax.numpy as jnp
import ml_dtypes
import numpy as np
from jax import lax
from jax.experimental import pallas as pl
from jax.experimental.pallas import tpu as pltpu
from jax.sharding import PartitionSpec as P

I = 1472
E = 64
K = 12
KT = 512
N = I + E
W = 2 * KT
RING = 8
WIDE = 64
LEV = 4
CHIPS = 128
LOC = 3
ROWS = 23
PAD = 24
COLS = 4
LAST = 5
M = K * COLS
MESH = pl.DeviceIdType.MESH
F32 = jnp.float32
BF16 = jnp.bfloat16


def wave_of(position):
    return np.where(position < KT, position, position + N - W)


def pair(table):
    high = table.astype(ml_dtypes.bfloat16)
    low = (table - high.astype(np.float64)).astype(ml_dtypes.bfloat16)
    depth, width = table.shape
    blocks = width // 128
    both = np.stack([high.reshape(depth, blocks, 128), low.reshape(depth, blocks, 128)], axis=2)
    return np.ascontiguousarray(both.transpose(1, 0, 2, 3).reshape(blocks, depth, 256))


@functools.lru_cache(maxsize=None)
def tables():
    position = np.arange(W)
    waves = wave_of(position)
    angle = 2.0 * np.pi / N * ((np.arange(N)[:, None] * waves[None, :]) % N)
    cas = np.cos(angle) + np.sin(angle)
    f = (np.arange(E) + 1.0) / (E + 1.0)
    h00, h10 = 2 * f**3 - 3 * f**2 + 1, f**3 - 2 * f**2 + f
    h01, h11 = -2 * f**3 + 3 * f**2, f**3 - f**2
    forward = cas[:I].copy()
    forward[I - 1] += (h00 + h10) @ cas[I:]
    forward[I - 2] -= h10 @ cas[I:]
    forward[0] += (h01 - h11) @ cas[I:]
    forward[1] += h11 @ cas[I:]
    inverse = cas[:I].T / N

    fx = np.zeros((N, W))
    fx[:I] = forward
    index, device = np.arange(N) // WIDE, np.arange(N) % WIDE
    good = index < ROWS
    source = np.where(good, ROWS * device + index, 0)
    fy = np.where(good[:, None], forward[source], 0.0)
    iy = np.where(good[None, :], inverse[:, source], 0.0)
    ix = np.zeros((W, N))
    ix[:, :I] = inverse
    ix = np.stack([pair(ix[: W // 2]), pair(ix[W // 2 :])])
    magnitude = np.minimum(waves, N - waves)
    lap = 4.0 * np.sin(np.pi * waves / N) ** 2
    line = np.zeros((8, W), np.float32)
    line[0], line[1] = lap, magnitude
    return pair(fx), pair(fy), pair(iy), ix, line


def split(value):
    high = value.astype(BF16)
    return high, (value - high.astype(F32)).astype(BF16)


def stack(value):
    high = value.astype(BF16).astype(F32)
    return jnp.concatenate([high, value - high], axis=0).astype(BF16)


def total(product, rows):
    return (
        (product[rows:, 128:] + product[:rows, 128:]) + product[rows:, :128]
    ) + product[:rows, :128]


def split_three(value):
    high, rest = value.astype(BF16), value
    rest = rest - high.astype(F32)
    middle = rest.astype(BF16)
    return high, middle, (rest - middle.astype(F32)).astype(BF16)


def kernel(
    x_hbm, to_hbm, from_hbm, depth_hbm, line_hbm, fx_hbm, fy_hbm, iy_hbm, ix_hbm, out_ref,
    x_ref, to_ref, from_ref, depth_ref, line_ref, fx, fy, iy, ix, xf, xs, ys, qs, ms, zs, part,
    swap_x, spec_x, send_a, recv_a, mid_a, mid_b, send_b, recv_b, home, other,
    in_sem, fx_sem, table_sem, swap_sem, s1_sem, s2_sem, r2_sem, s3_sem, r3_sem, all_sem,
):
    wide = lax.axis_index("wide")
    lev = lax.axis_index("lev")
    core = lev & 1
    half = lev >> 1
    ring = wide & (RING - 1)
    me = half * WIDE + wide
    partner = {"wide": wide, "lev": lev ^ 1}

    def chip(s):
        return {"wide": s & (WIDE - 1), "lev": ((s >> 6) << 1) + core}

    def across(q):
        return chip((q << 3) + ring)

    cross = me >> 3

    small = [
        pltpu.make_async_copy(source, target, in_sem.at[n])
        for n, (source, target) in enumerate(
            (
                (x_hbm, x_ref), (to_hbm, to_ref), (from_hbm, from_ref),
                (depth_hbm, depth_ref), (line_hbm, line_ref),
            )
        )
    ]
    small[0].start()

    blocks = [(core ^ 1) * COLS + c for c in range(COLS)] + [core * COLS + c for c in range(COLS)]
    fx_copies = []
    for n, block in enumerate(blocks):
        copy = pltpu.make_async_copy(fx_hbm.at[block], fx.at[n], fx_sem.at[n])
        copy.start()
        fx_copies.append(copy)
    rest = [
        pltpu.make_async_copy(source, target, table_sem.at[n])
        for n, (source, target) in enumerate(((fy_hbm, fy), (iy_hbm, iy), (ix_hbm, ix)))
    ]

    barrier = pltpu.get_barrier_semaphore()
    for step in range(1, RING):
        z = (ring + step) & (RING - 1)
        pl.semaphore_signal(
            barrier, inc=1, device_id=chip(me - ring + z), device_id_type=MESH
        )
    for step in range(1, 16):
        pl.semaphore_signal(
            barrier, inc=1, device_id=across((cross + step) & 15), device_id_type=MESH
        )
    pl.semaphore_signal(barrier, inc=1, device_id=partner, device_id_type=MESH)

    xf[...] = jnp.zeros_like(xf)
    small[0].wait()
    for l in range(LOC):
        xf[l * PAD : l * PAD + ROWS, :I] = x_ref[l]
    xs[...] = stack(xf[...])

    def swap_copy(c):
        return pltpu.make_async_remote_copy(
            src_ref=swap_x.at[c],
            dst_ref=spec_x.at[pl.ds(core * LOC, LOC), c],
            send_sem=s1_sem,
            recv_sem=swap_sem,
            device_id=partner,
            device_id_type=MESH,
        )

    for n in range(2 * COLS):
        fx_copies[n].wait()
        block = total(jnp.dot(xs[...], fx[n], preferred_element_type=F32), LOC * PAD)
        block = block.reshape(LOC, PAD, 128)
        if n < COLS:
            swap_x[n] = block
            if n == 0:
                pl.semaphore_wait(barrier, RING - 1 + 15 + 1)
                for step in range(1, 16):
                    pl.semaphore_signal(
                        all_sem, inc=1, device_id=across((cross + step) & 15), device_id_type=MESH
                    )
                for c in range(n):
                    swap_copy(c).start()
            if n >= 0:
                swap_copy(n).start()
        else:
            for l in range(LOC):
                spec_x[core * LOC + l, n - COLS] = block[l]

    for copy in small[1:] + rest:
        copy.start()

    def bulk(ref, sem):
        return pltpu.make_async_copy(ref, ref, sem)

    bulk(spec_x.at[pl.ds(0, LOC)], swap_sem).wait()

    def pack(rows, buffer):
        last = rows(LAST)
        for l in range(LAST):
            tail = last[32 * l : 32 * l + 32] if l < 3 else jnp.zeros((32, 128), F32)
            buffer[pl.ds(l, CHIPS, stride=8), :] = jnp.concatenate([rows(l), tail], axis=0).T

    def unpack(buffer, store):
        for l in range(LAST):
            rows = buffer[pl.ds(l, CHIPS, stride=8), :].T
            store(l, 0, rows[:96])
            if l < 3:
                store(LAST, 32 * l, rows[96:])

    pack(lambda l: spec_x[l].reshape(96, 128), send_a)

    def exchange(source, target, send_sem, recv_sem, between=None):
        def copy(s):
            return pltpu.make_async_remote_copy(
                src_ref=source.at[pl.ds(pl.multiple_of(s * 8, 8), LAST)],
                dst_ref=target.at[pl.ds(pl.multiple_of(me * 8, 8), LAST)],
                send_sem=send_sem,
                recv_sem=recv_sem,
                device_id=chip(s),
                device_id_type=MESH,
            )

        if between is not None:
            between()

        @pl.loop(1, CHIPS)
        def _(step):
            copy((me + step) & (CHIPS - 1)).start()

        own = pl.ds(pl.multiple_of(me * 8, 8), 8)
        target[own, :] = source[own, :]

    def arrived(buffer, sem):
        bulk(buffer.at[pl.ds(0, (CHIPS - 1) * LAST)], sem).wait()

    exchange(
        send_a, recv_a, s2_sem, r2_sem, between=lambda: pl.semaphore_wait(all_sem, 15)
    )

    row = lax.broadcasted_iota(jnp.int32, (M, 1), 0)
    pick = ((row >> 2) == lax.broadcasted_iota(jnp.int32, (M, K), 1)).astype(F32)
    turn = lax.broadcasted_iota(jnp.int32, (6 * M, 1), 0)
    turn = lax.rem(turn, M) >> 2
    pick_six = (turn == lax.broadcasted_iota(jnp.int32, (6 * M, K), 1)).astype(F32)
    lane = lax.broadcasted_iota(jnp.int32, (M, 6 * M), 1)
    same = (row & 3) == (lane & 3)

    def expand(small):
        tall = jnp.dot(pick, small, preferred_element_type=F32, precision=lax.Precision.HIGHEST)
        full = lax.dot_general(
            tall, pick_six, (((1,), (1,)), ((), ())),
            preferred_element_type=F32, precision=lax.Precision.HIGHEST,
        )
        full = jnp.where(same, full, 0.0)
        high = full.astype(BF16).astype(F32)
        middle = (full - high).astype(BF16).astype(F32)
        low = full - high - middle
        return jnp.where(lane < 3 * M, high, jnp.where(lane < 5 * M, middle, low)).astype(BF16)

    for copy in small[1:]:
        copy.wait()
    to_big = expand(to_ref[...])
    from_big = expand(from_ref[...])
    depth = jnp.sum(pick * depth_ref[...], axis=1, keepdims=True)
    column = core * (W // 2) + (row & 3) * CHIPS + me
    hit = lax.broadcasted_iota(jnp.int32, (M, W), 1) == column
    lap_q = jnp.sum(jnp.where(hit, line_ref[0:1], 0.0), axis=1, keepdims=True)
    mag_q = jnp.sum(jnp.where(hit, line_ref[1:2], 0.0), axis=1, keepdims=True)
    left = lax.broadcasted_iota(jnp.int32, (M // 2, 128), 1) < WIDE

    def triple(value, lanes):
        high, middle, low = split_three(value)
        for n, piece in enumerate((high, middle, low, high, middle, high)):
            qs[n * M : (n + 1) * M, lanes] = piece

    arrived(recv_a, r2_sem)

    def store_a(l, at, rows):
        mid_a[l * 96 + at : l * 96 + at + rows.shape[0]] = rows

    unpack(recv_a, store_a)
    for t in range(PAD // 2):
        a = mid_a[pl.ds(2 * t, M // 2, stride=PAD), :]
        b = mid_a[pl.ds(2 * t + 1, M // 2, stride=PAD), :]
        first = jnp.where(left, a, pltpu.roll(b, WIDE, 1))
        second = jnp.where(left, pltpu.roll(a, WIDE, 1), b)
        high, low = split(jnp.concatenate([first, second], axis=0))
        ys[:M, t * 128 : t * 128 + 128] = high
        ys[M:, t * 128 : t * 128 + 128] = low

    rest[0].wait()

    for j in range(W // 128):
        lanes = slice(j * 128, j * 128 + 128)
        triple(total(jnp.dot(ys[...], fy[j], preferred_element_type=F32), M), lanes)
    lap_p = line_ref[0:1]
    mag_p = line_ref[1:2]
    keep = (mag_p * mag_p + mag_q * mag_q < float(KT * KT)).astype(F32)
    modes = jnp.dot(to_big, qs[...], preferred_element_type=F32)
    triple(modes * keep / (1.0 + depth * (lap_p + lap_q)), slice(0, W))
    high, low = split(jnp.dot(from_big, qs[...], preferred_element_type=F32))
    ms[:M] = high
    ms[M:] = low

    rest[1].wait()
    for t in range(PAD // 2):
        value = total(jnp.dot(ms[...], iy[t], preferred_element_type=F32), M)
        first, second = value[: M // 2], value[M // 2 :]
        mid_b[pl.ds(2 * t, M // 2, stride=PAD), :] = jnp.where(
            left, first, pltpu.roll(second, WIDE, 1)
        )
        mid_b[pl.ds(2 * t + 1, M // 2, stride=PAD), :] = jnp.where(
            left, pltpu.roll(first, WIDE, 1), second
        )
    pack(lambda l: mid_b[l * 96 : l * 96 + 96], send_b)
    exchange(send_b, recv_b, s3_sem, r3_sem)
    rest[2].wait()
    arrived(recv_b, r3_sem)

    def store_b(l, at, rows):
        home[l, at : at + rows.shape[0]] = rows

    unpack(recv_b, store_b)
    back = pltpu.make_async_remote_copy(
        src_ref=home.at[pl.ds((core ^ 1) * LOC, LOC)],
        dst_ref=other,
        send_sem=table_sem.at[3],
        recv_sem=table_sem.at[4],
        device_id=partner,
        device_id_type=MESH,
    )
    back.start()

    def gather(level):
        for c in range(COLS):
            rows = [level(l)[PAD * c : PAD * c + PAD] for l in range(LOC)]
            zs[:, c * 128 : c * 128 + 128] = stack(jnp.concatenate(rows, axis=0))

    gather(lambda l: home[core * LOC + l])
    for j in range(N // 128):
        part[:, j * 128 : j * 128 + 128] = total(
            jnp.dot(zs[...], ix[core, j], preferred_element_type=F32), LOC * PAD
        )
    back.wait_recv()
    gather(lambda l: other[l])
    for j in range(N // 128):
        field = total(jnp.dot(zs[...], ix[core ^ 1, j], preferred_element_type=F32), LOC * PAD)
        field = field + part[:, j * 128 : j * 128 + 128]
        width = min(128, I - j * 128)
        for l in range(LOC):
            out_ref[l, :, j * 128 : j * 128 + width] = field[l * PAD : l * PAD + ROWS, :width]

    bulk(swap_x, s1_sem).wait()
    arrived(send_a, s2_sem)
    arrived(send_b, s3_sem)
    back.wait_send()


def shards(state_field, to_modes, from_modes, mode_depth):
    fx, fy, iy, ix, line = (jnp.asarray(table) for table in tables())
    hbm = pl.BlockSpec(memory_space=pl.ANY)
    dma = pltpu.SemaphoreType.DMA
    return pl.pallas_call(
        kernel,
        out_shape=pltpu.VMEM((LOC, ROWS, I), F32),
        in_specs=[hbm] * 9,
        out_specs=pl.BlockSpec(memory_space=pltpu.VMEM),
        scratch_shapes=[
            pltpu.VMEM((LOC, ROWS, I), F32),
            pltpu.VMEM((K, K), F32),
            pltpu.VMEM((K, K), F32),
            pltpu.VMEM((1, K), F32),
            pltpu.VMEM(line.shape, F32),
            pltpu.VMEM(fx.shape, BF16),
            pltpu.VMEM(fy.shape, BF16),
            pltpu.VMEM(iy.shape, BF16),
            pltpu.VMEM(ix.shape, BF16),
            pltpu.VMEM((LOC * PAD, N), F32),
            pltpu.VMEM((2 * LOC * PAD, N), BF16),
            pltpu.VMEM((2 * M, N), BF16),
            pltpu.VMEM((6 * M, W), BF16),
            pltpu.VMEM((2 * M, W), BF16),
            pltpu.VMEM((2 * LOC * PAD, W // 2), BF16),
            pltpu.VMEM((LOC * PAD, N), F32),
            pltpu.VMEM((COLS, LOC, PAD, 128), F32),
            pltpu.VMEM((2 * LOC, COLS, PAD, 128), F32),
            pltpu.VMEM((8 * CHIPS, 128), F32),
            pltpu.VMEM((8 * CHIPS, 128), F32),
            pltpu.VMEM((2 * LOC * 96, 128), F32),
            pltpu.VMEM((2 * LOC * 96, 128), F32),
            pltpu.VMEM((8 * CHIPS, 128), F32),
            pltpu.VMEM((8 * CHIPS, 128), F32),
            pltpu.VMEM((2 * LOC, 96, 128), F32),
            pltpu.VMEM((LOC, 96, 128), F32),
            dma((5,)),
            dma((2 * COLS,)),
            dma((5,)),
            dma,
            dma,
            dma,
            dma,
            dma,
            dma,
            pltpu.SemaphoreType.REGULAR,
        ],
        compiler_params=pltpu.CompilerParams(
            collective_id=0, has_side_effects=True, vmem_limit_bytes=56 * 2**20
        ),
        cost_estimate=pl.CostEstimate(flops=4 * 10**9, bytes_accessed=27 * 10**6, transcendentals=0),
    )(state_field, to_modes, from_modes, mode_depth.reshape(1, K), line, fx, fy, iy, ix)


def solution(mesh):
    assert dict(mesh.shape) == {"wide": WIDE, "lev": LEV}
    placed = (P("lev", "wide", None), P(), P(), P())
    return jax.shard_map(
        shards, mesh=mesh, in_specs=placed, out_specs=P("lev", "wide", None), check_vma=False
    )
```
